32 devices in a mesh: seq: 8 (over z, x), head: 4 (over y, core).
Axes of the slice: x: 2, y: 2, z: 4, core: 2. Of those that a mesh axis runs over, the one named last changes fastest.
Arguments:
- hidden_in: bfloat16 [32768, 1024], P('seq'), may hold values from -6 to 6
- norm_gain: bfloat16 [1024], replicated, may hold values from 0.099609375 to 1.8984375
- gate_weight: bfloat16 [1024, 2048], P(None, 'head'), may hold values from -0.1875 to 0.1875
- value_weight: bfloat16 [1024, 2048], P(None, 'head'), may hold values from -0.375 to 0.375
- state_weight: bfloat16 [1024, 256], replicated, may hold values from -0.1875 to 0.1875
- step_weight: bfloat16 [1024, 32], P(None, 'head'), may hold values from -0.1875 to 0.1875
- step_bias: float32 [32], P('head'), may hold values from -1 to 1
- decay_log: float32 [32], P('head'), may hold values from -16 to -3
- skip_gain: float32 [32], P('head'), may hold values from 0.5 to 1.5
- conv_value: bfloat16 [4, 2048], P(None, 'head'), may hold values from -3 to 3
- conv_state: bfloat16 [4, 256], replicated, may hold values from -3 to 3
- output_gain: bfloat16 [2048], P('head'), may hold values from 0.099609375 to 1.8984375
- output_weight: bfloat16 [2048, 1024], P('head'), may hold values from -0.125 to 0.125
- piece_lengths: int32 [16], replicated, may hold values from 1 to 16384, 32768 in all
Outputs:
- block_out: bfloat16 [32768, 1024], P(('seq', 'head'))
The draws below stay inside these ranges and needn't reach their ends.
Inputs may be any that keep to these rules, and one draw needn't show every extreme that they name: `piece_lengths`: the lengths sum to 32768; the pieces lie end to end from position 0.
All inputs are finite; a program needn't handle non-finite values.
Results may differ from the reference program's by a relative error of at most 0.018.
Values may be sent and summed in bfloat16 or wider, within the bound.
No kernel may reach another device: no remote copies, remote signals or barrier semaphores. Data moves between devices by JAX's collectives and lax.ppermute only.
A program may use at most 128 MiB of HBM per device.

```python
import math
import jax
import jax.numpy as jnp
import numpy as np
from jax import lax

D = 1024
HEADS = 32
HEAD_DIM = 64
STATE = 128
CONV = 4
BLOCK = 256
PIECES = 16
INNER = 2048
TOKENS = 32768


def draw_decay_log(key, part):
    slow_key = jax.random.fold_in(key, 11)
    fast_key = jax.random.fold_in(key, 12)
    pick_key = jax.random.fold_in(key, 13)
    slow_rates = jax.random.uniform(slow_key, (HEADS,), jnp.float32, math.log(0.2), math.log(1.5)) - math.log(TOKENS)
    fast_rates = jax.random.uniform(fast_key, (HEADS,), jnp.float32, math.log(0.02), math.log(0.04))
    fast_share = 0.5
    picked = jax.random.uniform(pick_key, (HEADS,), jnp.float32) < fast_share
    return jnp.where(picked, fast_rates, slow_rates).astype(jnp.float32)


def draw_value_weight(key, part):
    noise = jax.random.truncated_normal(key, -4.0, 4.0, (D, INNER), jnp.float32) / math.sqrt(D)
    column_ramp = 1.0 + jnp.arange(INNER, dtype=jnp.float32) / (INNER - 1)
    return (noise * column_ramp[None, :]).astype(jnp.bfloat16)


def block_levels(own_key, dims, split, smallest, largest):
    level, own = 1.0, jax.random.fold_in(own_key, 6)
    for axis_at, shards_of in split:
        steps = jnp.exp(jax.random.uniform(jax.random.fold_in(own, axis_at), (shards_of,), jnp.float32, smallest / len(split), largest / len(split)))
        level = level * jnp.repeat(steps, dims[axis_at] // shards_of).reshape([-1 if axis == axis_at else 1 for axis in range(len(dims))])
    return level


def profile(number_of, total, bound, slope):
    weights = [(1 << 20) // math.isqrt(grade ** slope) + 1 for grade in range(2, number_of + 1)]
    surplus, holding = total - bound - (number_of - 1), [1] * (number_of - 1)
    while surplus > 0:
        free = [i for i in range(number_of - 1) if holding[i] < bound]
        mass, remaining = sum([weights[i] for i in free]), surplus
        for i in free:
            more = min(bound - holding[i], max(1, remaining * weights[i] // mass), surplus)
            holding[i] = holding[i] + more
            surplus = surplus - more
    return np.array([bound] + holding)


def ragged(stream_key, number_of, total, bound, skew):
    if number_of == 2:
        one = jax.random.randint(stream_key, (), max(1, total - bound), min(bound, total - 1) + 1)
        return jnp.stack([one, total - one])
    tallies = jnp.asarray(profile(number_of, total, bound, skew), jnp.int32)
    couples = (number_of - 1) // 2
    giver, sink = tallies[1:1 + 2 * couples:2], tallies[2:2 + 2 * couples:2]
    slack = jnp.minimum(giver - 1, bound - sink)
    shifted = jax.random.randint(jax.random.fold_in(stream_key, 1), (couples,), 0, 1 << 20) % (slack + 1)
    tallies = tallies.at[1:1 + 2 * couples:2].set(giver - shifted).at[2:2 + 2 * couples:2].set(sink + shifted)
    return tallies[jax.random.permutation(jax.random.fold_in(stream_key, 2), number_of)]


def gaussian(stream_key, dims, scale, bound, pieces=(), kind=jnp.bfloat16):
    level = block_levels(stream_key, dims, pieces, -0.22, 0.18) if pieces else 1.0
    drawn = jax.random.normal(stream_key, dims, jnp.float32) * scale * level
    return jnp.minimum(jnp.maximum(drawn, -bound), bound).astype(kind)


def setup_inputs(seed: int = 0) -> dict:
    keys = jax.random.split(jax.random.key(seed), 15)
    return {
        "hidden_in": gaussian(keys[0], (TOKENS, D), 1.0, 6.0, ((0, 8),)),
        "norm_gain": jnp.clip(1.0 + 0.18 * jax.random.normal(keys[1], (D,), jnp.float32), 0.099609375, 1.8984375).astype(jnp.bfloat16),
        "gate_weight": gaussian(keys[2], (D, INNER), D ** -0.5, 0.1875, ((1, 4),)),
        "value_weight": draw_value_weight(jax.random.fold_in(keys[14], 71), 0),
        "state_weight": gaussian(keys[4], (D, 2 * STATE), D ** -0.5, 0.1875),
        "step_weight": gaussian(keys[5], (D, HEADS), D ** -0.5, 0.1875, ((1, 4),)),
        "step_bias": jnp.clip(jax.random.uniform(keys[6], (HEADS,), jnp.float32, -1.0, 1.0) * block_levels(keys[6], (HEADS,), ((0, 4),), -0.4, 0.0), -1.0, 1.0),
        "decay_log": draw_decay_log(jax.random.fold_in(keys[14], 71), 0),
        "skip_gain": jnp.clip(0.5 + 1.0 * jax.random.uniform(keys[8], (HEADS,), jnp.float32) ** block_levels(keys[8], (HEADS,), ((0, 4),), -0.2, 0.2), 0.5, 1.5),
        "conv_value": gaussian(keys[9], (CONV, INNER), CONV ** -0.5, 3.0, ((1, 4),)),
        "conv_state": gaussian(keys[10], (CONV, 2 * STATE), CONV ** -0.5, 3.0),
        "output_gain": jnp.clip(1.0 + 0.18 * jax.random.normal(keys[11], (INNER,), jnp.float32), 0.099609375, 1.8984375).astype(jnp.bfloat16),
        "output_weight": gaussian(keys[12], (INNER, D), INNER ** -0.5, 0.125, ((0, 4),)),
        "piece_lengths": ragged(keys[13], PIECES, TOKENS, TOKENS // 2, 2).astype(jnp.int32),
    }


exact_mode = lax.Precision.HIGHEST
epsilon = 1e-05

def rms_scale(values):
    return lax.rsqrt(lax.optimization_barrier(jnp.mean(values * values, axis=-1, keepdims=True)) + epsilon)

def piece_index(positions, piece_lengths):
    starts = jnp.cumsum(piece_lengths).astype(jnp.int32) - piece_lengths
    counted = lax.optimization_barrier(jnp.sum((starts[None, :] <= positions[:, None]).astype(jnp.int32), axis=1)).astype(jnp.int32)
    return counted - 1

def convolve(padded, padded_ids, kernel, length, reverse):
    tap_count = kernel.shape[0]
    centre_ids = padded_ids[tap_count - 1:tap_count - 1 + length]
    running = jnp.zeros((length, padded.shape[1]), jnp.float32)
    for offset in range(tap_count):
        start_row = 2 * (tap_count - 1) - offset if reverse else offset
        window = padded[start_row:start_row + length].astype(jnp.float32)
        same_piece = (padded_ids[start_row:start_row + length] == centre_ids)[:, None]
        running = running + jnp.where(same_piece, window * kernel[offset].astype(jnp.float32)[None, :], 0.0)
    return jax.nn.silu(running).astype(jnp.bfloat16)

def scan_direction(values, write_rows, read_rows, step_sizes, piece_ids, decay_log, skip_gain):
    length = values.shape[0]
    blocks = length // BLOCK
    head_total = step_sizes.shape[1]
    decay_rate = -jnp.exp(decay_log)
    row_iota = lax.broadcasted_iota(jnp.int32, (BLOCK, BLOCK), 0)
    col_iota = lax.broadcasted_iota(jnp.int32, (BLOCK, BLOCK), 1)
    lower_mask = row_iota >= col_iota

    def advance(carry, block_in):
        carried_state, prior_piece = carry
        block_values, block_write, block_read, block_steps, block_ids = block_in
        log_steps = block_steps * decay_rate[None, :]
        cumulative = jnp.cumsum(log_steps, axis=0)
        same_piece = lower_mask & (block_ids[:, None] == block_ids[None, :])
        log_gap = cumulative[:, None, :] - cumulative[None, :, :]
        decay_table = jnp.where(same_piece[:, :, None], jnp.exp(jnp.minimum(log_gap, 0.0)), 0.0)
        intersection = jnp.dot(block_read, block_write.T, preferred_element_type=jnp.float32)
        weight = (intersection[:, :, None] * decay_table * block_steps[None, :, :]).astype(jnp.bfloat16)
        values_wide = block_values.astype(jnp.float32).reshape(BLOCK, head_total, HEAD_DIM)
        local_mix = jnp.einsum('ijh,jhp->ihp', weight.astype(jnp.float32), values_wide)
        opening = jnp.where((block_ids == prior_piece)[:, None], jnp.exp(cumulative), 0.0)
        from_state = jnp.einsum('in,hpn->ihp', block_read.astype(jnp.float32), carried_state, precision=exact_mode)
        result = local_mix + from_state * opening[:, :, None] + skip_gain[None, :, None] * values_wide
        tail_weight = jnp.where((block_ids == block_ids[-1])[:, None], jnp.exp(cumulative[-1][None, :] - cumulative), 0.0) * block_steps
        fresh_state = jnp.einsum('jhp,jn->hpn', values_wide * tail_weight[:, :, None], block_write.astype(jnp.float32), precision=exact_mode)
        passing = jnp.where(block_ids[-1] == prior_piece, jnp.exp(cumulative[-1]), 0.0)
        next_state = passing[:, None, None] * carried_state + fresh_state
        return ((next_state, block_ids[-1]), result.reshape(BLOCK, head_total * HEAD_DIM).astype(jnp.bfloat16))
    initial = (jnp.zeros((head_total, HEAD_DIM, STATE), jnp.float32), jnp.array(-1, jnp.int32))
    blocks_in = (values.reshape(blocks, BLOCK, -1), write_rows.reshape(blocks, BLOCK, STATE), read_rows.reshape(blocks, BLOCK, STATE), step_sizes.reshape(blocks, BLOCK, head_total), piece_ids.reshape(blocks, BLOCK))
    final_carry, outputs = lax.scan(advance, initial, blocks_in)
    return outputs.reshape(length, -1)

def reference(hidden_in, norm_gain, gate_weight, value_weight, state_weight, step_weight, step_bias, decay_log, skip_gain, conv_value, conv_state, output_gain, output_weight, piece_lengths):
    wide_in = hidden_in.astype(jnp.float32)
    normed = (wide_in * rms_scale(wide_in) * norm_gain.astype(jnp.float32)[None, :]).astype(jnp.bfloat16)
    gate_rows = jnp.dot(normed, gate_weight, preferred_element_type=jnp.float32).astype(jnp.bfloat16)
    mixing_input = jnp.concatenate([jnp.dot(normed, value_weight, preferred_element_type=jnp.float32), jnp.dot(normed, state_weight, preferred_element_type=jnp.float32)], axis=1).astype(jnp.bfloat16)
    step_sizes = jax.nn.softplus(jnp.dot(normed, step_weight, preferred_element_type=jnp.float32) + step_bias[None, :])
    length = hidden_in.shape[0]
    positions = jnp.arange(length, dtype=jnp.int32)
    piece_ids = piece_index(positions, piece_lengths)
    kernel = jnp.concatenate([conv_value, conv_state], axis=1)
    margin = CONV - 1
    padded = jnp.pad(mixing_input, ((margin, margin), (0, 0)))
    padded_ids = jnp.pad(piece_ids, (margin, margin), constant_values=-2)
    forward_in = convolve(padded, padded_ids, kernel, length, False)
    backward_in = convolve(padded, padded_ids, kernel, length, True)
    inner_total = value_weight.shape[1]
    forward_out = scan_direction(forward_in[:, :inner_total], forward_in[:, inner_total:inner_total + STATE], forward_in[:, inner_total + STATE:], step_sizes, piece_ids, decay_log, skip_gain)
    flipped = jnp.flip(backward_in, 0)
    backward_out = jnp.flip(scan_direction(flipped[:, :inner_total], flipped[:, inner_total:inner_total + STATE], flipped[:, inner_total + STATE:], jnp.flip(step_sizes, 0), jnp.flip(piece_ids, 0), decay_log, skip_gain), 0)
    gate_wide = jax.nn.silu(gate_rows.astype(jnp.float32))
    gated_forward = forward_out.astype(jnp.float32) * gate_wide
    gated_backward = backward_out.astype(jnp.float32) * gate_wide
    combined = ((gated_forward * rms_scale(gated_forward) + gated_backward * rms_scale(gated_backward)) * output_gain.astype(jnp.float32)[None, :]).astype(jnp.bfloat16)
    return (wide_in + jnp.dot(combined, output_weight, preferred_element_type=jnp.float32)).astype(jnp.bfloat16)
```

```python
import functools

import jax
import jax.numpy as jnp
from jax import lax
from jax.experimental import pallas as pl
from jax.experimental.pallas import tpu as pltpu
from jax.sharding import PartitionSpec as P

HEAD_DIM = 64
STATE = 128
CONV = 4
BLOCK = 256
HALO = 16
LANES = 128
SAFE = 40.0
EPSILON = 1e-05
VMEM_LIMIT = 56 * 1024 * 1024

f32 = jnp.float32
bf16 = jnp.bfloat16


def dot(a, b):
    return jnp.dot(a, b, preferred_element_type=f32)


def dot_first(a, b):
    return lax.dot_general(a, b, (((0,), (0,)), ((), ())), preferred_element_type=f32)


def dot_last(a, b):
    return lax.dot_general(a, b, (((1,), (1,)), ((), ())), preferred_element_type=f32)


def iota(shape, dim):
    return lax.broadcasted_iota(jnp.int32, shape, dim)


def normalise(rows, gain):
    wide = rows.astype(f32)
    scale = lax.rsqrt(jnp.mean(wide * wide, axis=-1, keepdims=True) + EPSILON)
    return (wide * scale * gain).astype(bf16)


def split_halves(x):
    high = x.astype(bf16)
    low = (x - high.astype(f32)).astype(bf16)
    return high, low


def spread(factors, first, columns):
    pick = (iota((2 * LANES, columns), 0) & (LANES - 1)) == lax.div(
        iota((2 * LANES, columns), 1), HEAD_DIM
    ) + first
    return dot(factors, pick.astype(bf16))


def running_sum(x):
    lower = (iota((BLOCK, BLOCK), 0) >= iota((BLOCK, BLOCK), 1)).astype(bf16)
    high, low = split_halves(x)
    return dot(lower, high) + dot(lower, low)


def start_at(starts, count, row):
    found = starts[0]
    for k in range(1, count):
        s = starts[k]
        found = jnp.where(s <= row, jnp.maximum(found, s), found)
    return found


def start_after(starts, count, row):
    found = starts[count - 1]
    for k in range(count - 1):
        s = starts[k]
        found = jnp.where(s > row, jnp.minimum(found, s), found)
    return found


def has_cut(starts, count, low, high):
    found = jnp.int32(0)
    for k in range(count):
        s = starts[k]
        found = found | jnp.where((s >= low) & (s <= high), 1, 0)
    return found > 0


def row_bounds(starts, count, first):
    rows = iota((BLOCK, 1), 0) + first
    begin = jnp.zeros((BLOCK, 1), jnp.int32)
    end = jnp.zeros((BLOCK, 1), jnp.int32) + starts[count - 1]
    for k in range(count):
        s = starts[k]
        begin = jnp.where(s <= rows, jnp.maximum(begin, s), begin)
        end = jnp.where(s > rows, jnp.minimum(end, s), end)
    return rows, begin, end


def convolve(win, taps, columns, bounds, put):
    wide = LANES if columns % LANES == 0 else columns
    for at in range(0, columns, wide):
        cols = pl.ds(at, wide)

        def row(d):
            return win[pl.ds(HALO + d, BLOCK), cols]

        centre = taps[CONV - 1 : CONV, cols] * row(0)
        halves = []
        for sign in (-1, 1):
            total = centre
            for d in range(1, CONV):
                term = taps[CONV - 1 - d : CONV - d, cols] * row(sign * d)
                if bounds is not None:
                    rows, begin, end = bounds
                    inside = rows - d >= begin if sign < 0 else rows + d < end
                    term = jnp.where(inside, term, 0.0)
                total = total + term
            halves.append(total * jnp.tanh(total) + total)
        put(cols, halves[0], halves[1])


def convolve_block(win, taps, columns, starts, count, first, put):
    cut = has_cut(starts, count, first - (CONV - 2), first + BLOCK + CONV - 2)

    @pl.when(jnp.logical_not(cut))
    def _():
        convolve(win, taps, columns, None, put)

    @pl.when(cut)
    def _():
        convolve(win, taps, columns, row_bounds(starts, count, first), put)


def project_kernel(inner, heads, hidden, gain, value_w, state_w, step_w, bias, mix, steps, joined):
    @pl.when(pl.program_id(0) == 0)
    def _():
        joined[:, :inner] = value_w[...]
        joined[:, inner : inner + STATE] = state_w[...]
        joined[:, inner + STATE :] = step_w[...]

    normed = normalise(hidden[...], gain[...])
    out = dot(normed, joined[...])
    mix[...] = out[:, : inner + STATE].astype(bf16)
    raw = out[:, inner + STATE :] + bias[...]
    steps[...] = jnp.maximum(raw, 0.0) + jnp.log1p(jnp.exp(-jnp.abs(raw)))


def state_kernel(
    inner,
    count,
    places,
    info,
    mix,
    before,
    after,
    halo,
    gain,
    value_w,
    state_w,
    steps,
    rate,
    taps,
    ends,
    begins,
    passes,
    sent,
    edge,
    win,
    xf,
    xb,
    sums,
    total_f,
    total_b,
):
    quarter = pl.program_id(0)
    quarters = pl.num_programs(0)
    rows = mix.shape[0]
    blocks = rows // BLOCK
    columns = inner + STATE
    first = info[count] + quarter * rows

    @pl.when(quarter == 0)
    def _():
        normed = normalise(halo[...], gain[...])
        edge[:, :inner] = dot(normed, value_w[...]).astype(bf16).astype(f32)
        edge[:, inner:] = dot(normed, state_w[...]).astype(bf16).astype(f32)
        total_f[...] = jnp.zeros_like(total_f)
        total_b[...] = jnp.zeros_like(total_b)
        total_b[STATE : STATE + 1] = jnp.ones((1, inner), f32)
        total_f[STATE : STATE + 1] = jnp.ones((1, inner), f32)

    total = jnp.zeros((1, LANES), f32)
    for c in range(blocks):
        at = pl.ds(c * BLOCK, BLOCK)
        part = running_sum(-steps[at, :] * rate[...]) + total
        sums[at, :] = part
        total = part[BLOCK - 1 : BLOCK]

    last_start = start_at(info, count, first + rows - 1)
    first_end = start_after(info, count, first)

    end_state = jnp.zeros((STATE, inner), f32)
    begin_state = jnp.zeros((STATE, inner), f32)
    for c in range(blocks):
        at = pl.ds(c * BLOCK, BLOCK)
        win[HALO : HALO + BLOCK, :] = mix[at, :].astype(f32)
        if c == 0:
            win[:HALO, :] = jnp.where(quarter == 0, edge[:HALO], before[...].astype(f32))
        else:
            win[:HALO, :] = mix[c * BLOCK - HALO : c * BLOCK, :].astype(f32)
        if c == blocks - 1:
            win[HALO + BLOCK :, :] = jnp.where(
                quarter == quarters - 1, edge[HALO:], after[...].astype(f32)
            )
        else:
            win[HALO + BLOCK :, :] = mix[(c + 1) * BLOCK : (c + 1) * BLOCK + HALO, :].astype(f32)

        def put(cols, forward, backward):
            xf[:, cols] = forward
            xb[:, cols] = backward

        here = first + c * BLOCK
        convolve_block(win, taps, columns, info, count, here, put)
        dt = steps[at, :]
        inclusive = sums[at, :]
        weight_f = dt * jnp.exp(total - inclusive)
        weight_b = dt * jnp.exp(inclusive + dt * rate[...])
        position = iota((BLOCK, 1), 0) + here
        spread_f = spread(jnp.concatenate(split_halves(weight_f), axis=1), 0, inner)
        spread_b = spread(jnp.concatenate(split_halves(weight_b), axis=1), 0, inner)
        write_f = jnp.where(position >= last_start, xf[:, inner:], 0.0).astype(bf16)
        write_b = jnp.where(position < first_end, xb[:, inner:], 0.0).astype(bf16)
        end_state += dot_first(write_f, (xf[:, :inner] * spread_f).astype(bf16))
        begin_state += dot_first(write_b, (xb[:, :inner] * spread_b).astype(bf16))

    ends[0] = end_state
    begins[0] = begin_state
    decay = spread(
        jnp.concatenate(split_halves(jnp.broadcast_to(jnp.exp(total), (8, LANES))), axis=1), 0, inner
    )
    pass_f = jnp.where(last_start < first, decay, 0.0)
    pass_b = jnp.where(first_end > first + rows, decay, 0.0)
    passes[0, :8] = pass_f
    passes[0, 8:] = pass_b
    through_f = total_f[STATE : STATE + 1]
    through_b = total_b[STATE : STATE + 1]
    total_f[:STATE] = pass_f[:1] * total_f[:STATE] + end_state
    total_b[:STATE] = total_b[:STATE] + through_b * begin_state
    total_f[STATE : STATE + 1] = through_f * pass_f[:1]
    total_b[STATE : STATE + 1] = through_b * pass_b[:1]

    @pl.when(quarter == quarters - 1)
    def _():
        place = info[count + 1]
        for total_ref, later in ((total_f, True), (total_b, False)):
            state = total_ref[:STATE].astype(bf16)
            high, low = split_halves(total_ref[STATE : STATE + 1])
            pad = jnp.zeros((HALO - 2, inner), f32)
            extra = jnp.concatenate([high.astype(f32), low.astype(f32), pad], axis=0).astype(bf16)

            def fill(p, carry):
                @pl.when((p > place) if later else (p <= place))
                def _():
                    sent[p, :STATE] = state
                    sent[p, STATE:] = extra

                return carry

            lax.fori_loop(0, places, fill, 0)


def carry_kernel(places, quarters, count, info, got, ends, begins, passes, out):
    place = info[count + 1]
    shape = ends.shape[1:]

    def step(p, state):
        decay = got[p, STATE : STATE + HALO].astype(f32)
        return (decay[0:1] + decay[1:2]) * state + got[p, :STATE].astype(f32)

    def forward(p, state):
        return step(p, state)

    def backward(p, state):
        return step(places - 1 - p, state)

    state = lax.fori_loop(0, place, forward, jnp.zeros(shape, f32))
    for q in range(quarters):
        out[q, 0] = state.astype(bf16)
        state = passes[q, 0:1] * state + ends[q]
    state = lax.fori_loop(0, places - 1 - place, backward, jnp.zeros(shape, f32))
    for q in reversed(range(quarters)):
        out[q, 1] = state.astype(bf16)
        state = passes[q, 8:9] * state + begins[q]


def shared_kernel(
    heads,
    count,
    info,
    hidden,
    gain,
    state_w,
    step_w,
    bias,
    rate,
    taps,
    normed_out,
    factors,
    reach,
    raw,
    raw_t,
    mix_f,
    mix_b,
    write_f,
    write_b,
    read_f,
    read_b,
    enter_f,
    enter_b,
    flags,
    wide,
    win,
    xf,
    xb,
):
    rows = hidden.shape[0] - 2 * HALO
    blocks = rows // BLOCK
    first = info[count + 2]
    normed_out[...] = normalise(hidden[...], gain[...])
    wide[...] = dot(normed_out[...], state_w[...]).astype(bf16).astype(f32)
    kind = lax.div(iota((1, LANES), 1), heads)
    totals = []
    for c in range(blocks):
        at = pl.ds(c * BLOCK, BLOCK)
        step_raw = dot(normed_out[pl.ds(HALO + c * BLOCK, BLOCK), :], step_w[...]) + bias[...]
        dt = jnp.maximum(step_raw, 0.0) + jnp.log1p(jnp.exp(-jnp.abs(step_raw)))
        log_step = -dt * rate[...]
        upto = running_sum(log_step)
        total = upto[BLOCK - 1 : BLOCK]
        onward = total - upto + log_step
        totals.append(total)
        flags[c] = jnp.where(jnp.max(-total) > SAFE, 1, 0)
        value = jnp.where(kind == 0, upto, jnp.where(kind == 1, dt, jnp.where(kind == 2, onward, total)))
        raw[at, :] = value
        raw_t[c] = jnp.transpose(value)
        power = jnp.where(
            kind == 0, upto, jnp.where(kind == 1, -upto, jnp.where(kind == 2, onward, -onward))
        )
        factor = jnp.exp(jnp.minimum(power, SAFE)) * jnp.where((kind & 1) == 1, dt, 1.0)
        factors[at, :] = jnp.concatenate(split_halves(factor), axis=1)

    zero = jnp.zeros((1, LANES), f32)
    ahead = [zero]
    for c in range(blocks - 1):
        ahead.append(ahead[-1] + totals[c])
    behind = [zero]
    for c in reversed(range(1, blocks)):
        behind.insert(0, behind[0] + totals[c])
    quarter_end = start_after(info, count, first - 1)
    quarter_start = start_at(info, count, first + rows)
    for c in range(blocks):
        at = pl.ds(c * BLOCK, BLOCK)
        value = raw[at, :]
        power = jnp.where(kind == 0, value + ahead[c], value + behind[c])
        factor = jnp.where((kind & 1) == 0, jnp.exp(jnp.minimum(power, 0.0)), 0.0)
        reach[at, :] = jnp.concatenate(split_halves(factor), axis=1)

        here = first + c * BLOCK
        win[...] = wide[pl.ds(c * BLOCK, BLOCK + 2 * HALO), :]

        def put(cols, forward, backward):
            xf[:, cols] = forward
            xb[:, cols] = backward

        convolve_block(win, taps, 2 * STATE, info, count, here, put)
        position, begin, end = row_bounds(info, count, here)
        other = iota((BLOCK, BLOCK), 1) + here
        for x, mix, write, read, enter, ahead_of in (
            (xf, mix_f, write_f, read_f, enter_f, True),
            (xb, mix_b, write_b, read_b, enter_b, False),
        ):
            writes = x[:, :STATE]
            reads = x[:, STATE:]
            inner_product = dot_last(reads.astype(bf16), writes.astype(bf16))
            if ahead_of:
                allowed = (other <= position) & (other >= begin)
                keep = position >= start_at(info, count, here + BLOCK - 1)
                opened = position < start_after(info, count, here - 1)
                entered = position < quarter_end
            else:
                allowed = (other >= position) & (other < end)
                keep = position < start_after(info, count, here)
                opened = position >= start_at(info, count, here + BLOCK)
                entered = position >= quarter_start
            mix[c] = jnp.where(allowed, inner_product, 0.0).astype(bf16)
            write[at, :] = jnp.where(keep, writes, 0.0).astype(bf16)
            read[at, :] = jnp.where(opened, reads, 0.0).astype(bf16)
            enter[at, :] = jnp.where(entered, reads, 0.0).astype(bf16)


def group_kernel(
    group,
    group_heads,
    heads,
    count,
    info,
    flags,
    normed,
    value_w,
    gate_w,
    taps,
    skip,
    factors,
    raw,
    raw_t,
    mix_f,
    mix_b,
    write_f,
    write_b,
    read_f,
    read_b,
    out_f,
    out_b,
    gate_out,
    win,
    xf,
    xb,
    acc,
    state,
):
    inner = value_w.shape[1]
    rows = out_f.shape[0]
    blocks = rows // BLOCK
    first = info[count + 2]
    offset = group * group_heads

    def direction(c, x, mix, write, read, out, kind, edge_row, passing):
        at = pl.ds(pl.multiple_of(c * BLOCK, BLOCK), BLOCK)
        here_factors = factors[at, :]
        grow = spread(here_factors, kind * heads + offset, inner)
        decay = grow[edge_row : edge_row + 1]
        through = jnp.where(passing, 1.0, 0.0)
        flag = flags[c]
        carried = state[...]
        from_state = dot(read[at, :], carried.astype(bf16))

        @pl.when(flag == 0)
        def _():
            scaled = (x[...] * spread(here_factors, (kind + 1) * heads + offset, inner)).astype(bf16)
            total = dot(mix[c], scaled) + from_state
            out[at, :] = (total * grow + skip[...] * x[...]).astype(bf16)
            state[...] = decay * (dot_first(write[at, :], scaled) + through * carried)

        @pl.when(flag != 0)
        def _():
            pairs = mix[c].astype(f32)
            lane = iota((1, LANES), 1)
            half = iota((1, LANES), 1) >= HEAD_DIM
            values = raw[at, :]

            def pair(p, unused):
                cols = pl.ds(pl.multiple_of(p * LANES, LANES), LANES)
                x_pair = x[:, cols].astype(bf16)
                sums = []
                for side in range(LANES // HEAD_DIM):
                    head = kind * heads + offset + p * (LANES // HEAD_DIM) + side
                    down = jnp.sum(jnp.where(lane == head, values, 0.0), axis=1, keepdims=True)
                    across = raw_t[c, pl.ds(head, 1), :]
                    head_steps = raw_t[c, pl.ds(head - kind * heads + heads, 1), :]
                    table = pairs * jnp.exp(jnp.minimum(down - across, 0.0)) * head_steps
                    sums.append(dot(table.astype(bf16), x_pair))
                acc[:, cols] = jnp.where(half, sums[1], sums[0])
                return unused

            lax.fori_loop(0, inner // LANES, pair, 0)
            out[at, :] = (acc[...] + grow * from_state + skip[...] * x[...]).astype(bf16)
            edge_values = values[edge_row : edge_row + 1]
            step_lane = pltpu.roll(values, (kind - 1) * heads % LANES, 1)
            weight = jnp.where(
                lax.div(lane, heads) == kind,
                step_lane * jnp.exp(jnp.minimum(edge_values - values, 0.0)),
                0.0,
            )
            weights = jnp.concatenate(split_halves(weight), axis=1)
            scaled = (x[...] * spread(weights, kind * heads + offset, inner)).astype(bf16)
            state[...] = dot_first(write[at, :], scaled) + through * decay * carried

    state[...] = jnp.zeros_like(state)

    def ascend(c, unused):
        near = pl.ds(pl.multiple_of(c * BLOCK, BLOCK), BLOCK + 2 * HALO)
        at = pl.ds(pl.multiple_of(c * BLOCK, BLOCK), BLOCK)
        here = first + c * BLOCK
        rows_here = normed[near, :]
        win[...] = dot(rows_here, value_w[...]).astype(bf16).astype(f32)
        gate = dot(rows_here[HALO : HALO + BLOCK], gate_w[...]).astype(bf16).astype(f32) * 0.5
        gate_out[at, :] = (gate * jnp.tanh(gate) + gate).astype(bf16)

        def put(cols, forward, backward):
            xf[:, cols] = forward
            xb[c, :, cols] = backward

        convolve_block(win, taps, inner, info, count, here, put)
        passing = start_at(info, count, here + BLOCK - 1) < here
        direction(c, xf, mix_f, write_f, read_f, out_f, 0, BLOCK - 1, passing)
        return unused

    lax.fori_loop(0, blocks, ascend, 0)
    state[...] = jnp.zeros_like(state)

    def descend(k, unused):
        c = blocks - 1 - k
        here = first + c * BLOCK
        passing = start_after(info, count, here) > here + BLOCK
        direction(c, xb.at[c], mix_b, write_b, read_b, out_b, 2, 0, passing)
        return unused

    lax.fori_loop(0, blocks, descend, 0)


def finish_kernel(groups, group_heads, heads, count, info, *refs):
    hidden, reach, enter_f, enter_b, carries, gains = refs[:6]
    refs = refs[6:]
    out_f, out_b, gates, weights = (refs[k * groups : (k + 1) * groups] for k in range(4))
    out, held_f, held_b = refs[4 * groups :]
    me = info[count + 3]
    inner = weights[0].shape[0]
    here_reach = reach[...]
    sums = [jnp.zeros((BLOCK, 1), f32), jnp.zeros((BLOCK, 1), f32)]
    for g in range(groups):
        gate = gates[g][...].astype(f32)
        for k, (base, enter, held) in enumerate(((out_f, enter_f, held_f), (out_b, enter_b, held_b))):
            grow = spread(here_reach, 2 * k * heads + g * group_heads, inner)
            full = base[g][...].astype(f32) + grow * dot(enter[...], carries[me ^ g, k])
            gated = full * gate
            held[:, g * inner : (g + 1) * inner] = gated
            sums[k] = sums[k] + jnp.sum(gated * gated, axis=1, keepdims=True)
    scale_f, scale_b = (lax.rsqrt(s / (groups * inner) + EPSILON) for s in sums)
    total = hidden[...].astype(f32)
    for g in range(groups):
        cols = slice(g * inner, (g + 1) * inner)
        combined = (held_f[:, cols] * scale_f + held_b[:, cols] * scale_b) * gains[g : g + 1]
        total = total + dot(combined.astype(bf16), weights[g][...])
    out[...] = total.astype(bf16)


def whole(shape):
    return pl.BlockSpec(shape, lambda *_: (0,) * len(shape))


def struct(shape, dtype):
    return jax.ShapeDtypeStruct(shape, dtype)


def call(kernel, grid, scalars, arrays, in_specs, out_shape, out_specs, scratch, name):
    return pl.pallas_call(
        kernel,
        grid_spec=pltpu.PrefetchScalarGridSpec(
            num_scalar_prefetch=len(scalars),
            grid=grid,
            in_specs=in_specs,
            out_specs=out_specs,
            scratch_shapes=scratch,
        ),
        out_shape=out_shape,
        compiler_params=pltpu.CompilerParams(
            dimension_semantics=("arbitrary",) * len(grid), vmem_limit_bytes=VMEM_LIMIT
        ),
        name=name,
    )(*scalars, *arrays)


def swap(x, axis, distance):
    return lax.ppermute(x, axis, [(i, i ^ distance) for i in range(lax.axis_size(axis))])


def gather_near(x, groups):
    held = [None] * groups
    held[0] = x
    for k in range(2, groups, 2):
        held[k] = swap(x, "head", k)
    for k in range(1, groups, 2):
        held[k] = swap(held[k - 1], "head", 1)
    return held


def local(
    hidden_in,
    norm_gain,
    gate_weight,
    value_weight,
    state_weight,
    step_weight,
    step_bias,
    decay_log,
    skip_gain,
    conv_value,
    conv_state,
    output_gain,
    output_weight,
    piece_lengths,
):
    tokens, width = hidden_in.shape
    group_heads = step_bias.shape[0]
    inner = value_weight.shape[1]
    groups = lax.axis_size("head")
    places = lax.axis_size("seq")
    heads = group_heads * groups
    me = lax.axis_index("head")
    place = lax.axis_index("seq")
    rows = tokens // groups
    blocks = rows // BLOCK
    count = piece_lengths.shape[0] + 1

    up = [(i, i + 1) for i in range(places - 1)]
    down = [(i + 1, i) for i in range(places - 1)]
    before = lax.ppermute(hidden_in[-HALO:], "seq", up)
    after = lax.ppermute(hidden_in[:HALO], "seq", down)
    values = gather_near(value_weight, groups)
    gates = gather_near(gate_weight, groups)
    outs = gather_near(output_weight, groups)
    packed = jnp.concatenate(
        [
            conv_value.astype(f32).reshape(-1),
            output_gain.astype(f32),
            step_weight.astype(f32).reshape(-1),
            step_bias,
            decay_log,
            skip_gain,
        ]
    )
    packed = lax.all_gather(packed, "head")
    packed = jnp.take(packed, me ^ jnp.arange(groups), axis=0)
    cuts = [CONV * inner, inner, width * group_heads, group_heads, group_heads, group_heads]
    parts, at = [], 0
    for size in cuts:
        parts.append(packed[:, at : at + size])
        at += size
    taps_all = parts[0].reshape(groups, CONV, inner) * 0.5
    gains_all = parts[1]
    step_all = jnp.transpose(parts[2].reshape(groups, width, group_heads), (1, 0, 2)).reshape(width, heads)
    kinds = LANES // heads
    step_all = jnp.tile(step_all.astype(bf16), (1, kinds))
    bias_all = jnp.tile(parts[3].reshape(1, heads), (1, kinds))
    rate_all = jnp.tile(jnp.exp(parts[4]).reshape(1, heads), (1, kinds))
    skip_all = jnp.repeat(parts[5], HEAD_DIM, axis=1)

    starts = jnp.concatenate([jnp.zeros((1,), jnp.int32), jnp.cumsum(piece_lengths).astype(jnp.int32)])
    info = jnp.concatenate(
        [
            starts,
            jnp.stack([place * tokens, place, place * tokens + me * rows, me]).astype(jnp.int32),
        ]
    )
    gain = norm_gain.astype(f32).reshape(1, width)
    pad = ((0, 0), (0, LANES - group_heads))
    taps_own = jnp.concatenate([conv_value, conv_state[:, :STATE]], axis=1).astype(f32) * 0.5

    tile = min(512, rows)
    columns = inner + STATE
    mix, steps = call(
        functools.partial(project_kernel, inner, group_heads),
        (tokens // tile,),
        (),
        (
            hidden_in,
            gain,
            value_weight,
            state_weight,
            jnp.pad(step_weight, pad),
            jnp.pad(step_bias.reshape(1, -1), pad),
        ),
        [
            pl.BlockSpec((tile, width), lambda i: (i, 0)),
            whole((1, width)),
            whole((width, inner)),
            whole((width, STATE)),
            whole((width, LANES)),
            whole((1, LANES)),
        ],
        [struct((tokens, columns), bf16), struct((tokens, LANES), f32)],
        [pl.BlockSpec((tile, columns), lambda i: (i, 0)), pl.BlockSpec((tile, LANES), lambda i: (i, 0))],
        [pltpu.VMEM((width, columns + LANES), bf16)],
        "project",
    )
    per = rows // HALO
    ends, begins, passes, sent = call(
        functools.partial(state_kernel, inner, count, places),
        (groups,),
        (info,),
        (
            mix,
            mix,
            mix,
            jnp.concatenate([before, after]),
            gain,
            value_weight,
            state_weight,
            steps,
            jnp.pad(jnp.exp(decay_log).reshape(1, -1), pad),
            taps_own,
        ),
        [
            pl.BlockSpec((rows, columns), lambda i, _: (i, 0)),
            pl.BlockSpec((HALO, columns), lambda i, _: (jnp.maximum(i * per - 1, 0), 0)),
            pl.BlockSpec(
                (HALO, columns), lambda i, _: (jnp.minimum((i + 1) * per, tokens // HALO - 1), 0)
            ),
            whole((2 * HALO, width)),
            whole((1, width)),
            whole((width, inner)),
            whole((width, STATE)),
            pl.BlockSpec((rows, LANES), lambda i, _: (i, 0)),
            whole((1, LANES)),
            whole((CONV, columns)),
        ],
        [
            struct((groups, STATE, inner), f32),
            struct((groups, STATE, inner), f32),
            struct((groups, 16, inner), f32),
            struct((places, STATE + HALO, inner), bf16),
        ],
        [
            pl.BlockSpec((1, STATE, inner), lambda i, _: (i, 0, 0)),
            pl.BlockSpec((1, STATE, inner), lambda i, _: (i, 0, 0)),
            pl.BlockSpec((1, 16, inner), lambda i, _: (i, 0, 0)),
            whole((places, STATE + HALO, inner)),
        ],
        [
            pltpu.VMEM((2 * HALO, columns), f32),
            pltpu.VMEM((BLOCK + 2 * HALO, columns), f32),
            pltpu.VMEM((BLOCK, columns), f32),
            pltpu.VMEM((BLOCK, columns), f32),
            pltpu.VMEM((rows, LANES), f32),
            pltpu.VMEM((STATE + 8, inner), f32),
            pltpu.VMEM((STATE + 8, inner), f32),
        ],
        "states",
    )
    got = lax.all_to_all(sent, "seq", split_axis=0, concat_axis=0, tiled=True)

    own_first = me * rows
    own = lax.dynamic_slice_in_dim(hidden_in, own_first, rows, 0)
    above = lax.dynamic_slice_in_dim(hidden_in, jnp.maximum(own_first - HALO, 0), HALO, 0)
    below = lax.dynamic_slice_in_dim(hidden_in, jnp.minimum(own_first + rows, tokens - HALO), HALO, 0)
    near = jnp.concatenate(
        [jnp.where(me == 0, before, above), own, jnp.where(me == groups - 1, after, below)]
    )
    long = rows + 2 * HALO
    square = struct((blocks, BLOCK, BLOCK), bf16)
    thin = struct((rows, STATE), bf16)
    shapes = [
        struct((long, width), bf16),
        struct((rows, 2 * LANES), bf16),
        struct((rows, 2 * LANES), bf16),
        struct((rows, LANES), f32),
        struct((blocks, LANES, BLOCK), f32),
        square,
        square,
        thin,
        thin,
        thin,
        thin,
        thin,
        thin,
        struct((blocks,), jnp.int32),
    ]
    shared = call(
        functools.partial(shared_kernel, heads, count),
        (1,),
        (info,),
        (near, gain, state_weight, step_all, bias_all, rate_all, conv_state.astype(f32) * 0.5),
        [
            whole((long, width)),
            whole((1, width)),
            whole((width, 2 * STATE)),
            whole((width, LANES)),
            whole((1, LANES)),
            whole((1, LANES)),
            whole((CONV, 2 * STATE)),
        ],
        shapes,
        [whole(s.shape) for s in shapes[:-1]] + [pl.BlockSpec(memory_space=pltpu.SMEM)],
        [
            pltpu.VMEM((long, 2 * STATE), f32),
            pltpu.VMEM((BLOCK + 2 * HALO, 2 * STATE), f32),
            pltpu.VMEM((BLOCK, 2 * STATE), f32),
            pltpu.VMEM((BLOCK, 2 * STATE), f32),
        ],
        "shared",
    )
    normed, factors, reach, raw, raw_t, mix_f, mix_b, write_f, write_b, read_f, read_b = shared[:11]
    enter_f, enter_b, flags = shared[11:]
    outs_f, outs_b, gate_rows = [], [], []
    for g in range(groups):
        arrays = (
            normed,
            values[g],
            gates[g],
            taps_all[g],
            skip_all[g : g + 1],
            factors,
            raw,
            raw_t,
            mix_f,
            mix_b,
            write_f,
            write_b,
            read_f,
            read_b,
        )
        done = call(
            functools.partial(group_kernel, g, group_heads, heads, count),
            (1,),
            (info, flags),
            arrays,
            [whole(a.shape) for a in arrays],
            [struct((rows, inner), bf16)] * 3,
            [whole((rows, inner))] * 3,
            [
                pltpu.VMEM((BLOCK + 2 * HALO, inner), f32),
                pltpu.VMEM((BLOCK, inner), f32),
                pltpu.VMEM((blocks, BLOCK, inner), f32),
                pltpu.VMEM((BLOCK, inner), f32),
                pltpu.VMEM((STATE, inner), f32),
            ],
            "group%d" % g,
        )
        outs_f.append(done[0])
        outs_b.append(done[1])
        gate_rows.append(done[2])

    entering = call(
        functools.partial(carry_kernel, places, groups, count),
        (1,),
        (info,),
        (got, ends, begins, passes),
        [whole(a.shape) for a in (got, ends, begins, passes)],
        struct((groups, 2, STATE, inner), bf16),
        whole((groups, 2, STATE, inner)),
        [],
        "carries",
    )
    carries = lax.all_to_all(entering, "head", split_axis=0, concat_axis=0, tiled=True)

    def by_block(columns):
        return pl.BlockSpec((BLOCK, columns), lambda i, _: (i, 0))

    return call(
        functools.partial(finish_kernel, groups, group_heads, heads, count),
        (blocks,),
        (info,),
        (own, reach, enter_f, enter_b, carries, gains_all, *outs_f, *outs_b, *gate_rows, *outs),
        [
            by_block(width),
            by_block(2 * LANES),
            by_block(STATE),
            by_block(STATE),
            whole(carries.shape),
            whole(gains_all.shape),
        ]
        + [by_block(inner)] * (3 * groups)
        + [whole((inner, width))] * groups,
        struct((rows, width), bf16),
        by_block(width),
        [pltpu.VMEM((BLOCK, groups * inner), f32), pltpu.VMEM((BLOCK, groups * inner), f32)],
        "finish",
    )


def solution(mesh):
    in_specs = (
        P("seq", None),
        P(),
        P(None, "head"),
        P(None, "head"),
        P(),
        P(None, "head"),
        P("head"),
        P("head"),
        P("head"),
        P(None, "head"),
        P(),
        P("head"),
        P("head", None),
        P(),
    )
    out_specs = P(("seq", "head"), None)
    return jax.shard_map(local, mesh=mesh, in_specs=in_specs, out_specs=out_specs, check_vma=False)
```

```python
import functools

import jax
import jax.numpy as jnp
from jax import lax
from jax.experimental import pallas as pl
from jax.experimental.pallas import tpu as pltpu
from jax.sharding import PartitionSpec as P

HEAD_DIM = 64
STATE = 128
CONV = 4
BLOCK = 256
HALO = 16
SUB = 8
SPAN = BLOCK // SUB + 1
COVER = SPAN * SUB
WINDOW = BLOCK + 2 * HALO
LANES = 128
SAFE = 40.0
EPSILON = 1e-05
VMEM_LIMIT = 56 * 1024 * 1024

f32 = jnp.float32
bf16 = jnp.bfloat16


def dot(a, b):
    return jnp.dot(a, b, preferred_element_type=f32)


def dot_first(a, b):
    return lax.dot_general(a, b, (((0,), (0,)), ((), ())), preferred_element_type=f32)


def dot_last(a, b):
    return lax.dot_general(a, b, (((1,), (1,)), ((), ())), preferred_element_type=f32)


def iota(shape, dim):
    return lax.broadcasted_iota(jnp.int32, shape, dim)


def normalise(rows, gain):
    wide = rows.astype(f32)
    scale = lax.rsqrt(jnp.mean(wide * wide, axis=-1, keepdims=True) + EPSILON)
    return (wide * scale * gain).astype(bf16)


def split_halves(x):
    high = x.astype(bf16)
    low = (x - high.astype(f32)).astype(bf16)
    return high, low


def picks(first, columns):
    shape = (2 * LANES, columns)
    pick = (iota(shape, 0) & (LANES - 1)) == lax.div(iota(shape, 1), HEAD_DIM) + first
    return pick.astype(bf16)


def side_by_side(tiles):
    return jnp.concatenate([tiles[k, :BLOCK] for k in range(tiles.shape[0])], axis=1)


def tile_up(tiles, at, x):
    for k in range(tiles.shape[0]):
        tiles[k, at] = x[:, k * LANES : (k + 1) * LANES]


def halves_of(x):
    return jnp.concatenate(split_halves(x), axis=1)


def running_sum(x):
    lower = (iota((BLOCK, BLOCK), 0) >= iota((BLOCK, BLOCK), 1)).astype(bf16)
    high, low = split_halves(x)
    return dot(lower, high) + dot(lower, low)


def bounds_of(lengths, pieces):
    starts = [jnp.int32(0)]
    for k in range(pieces):
        starts.append(starts[-1] + lengths[k])
    return starts


def start_at(starts, row):
    found = starts[0]
    for s in starts[1:]:
        found = jnp.where(s <= row, jnp.maximum(found, s), found)
    return found


def start_after(starts, row):
    found = starts[-1]
    for s in starts[:-1]:
        found = jnp.where(s > row, jnp.minimum(found, s), found)
    return found


def has_cut(starts, low, high):
    found = jnp.int32(0)
    for s in starts:
        found = found | jnp.where((s >= low) & (s <= high), 1, 0)
    return found > 0


def piece_bounds(starts, rows):
    begin = jnp.zeros(rows.shape, jnp.int32)
    end = jnp.zeros(rows.shape, jnp.int32) + starts[-1]
    for s in starts:
        begin = jnp.where(s <= rows, jnp.maximum(begin, s), begin)
        end = jnp.where(s > rows, jnp.minimum(end, s), end)
    return begin, end


def convolve(win, offset, taps, room, put):
    offset = offset + HALO
    for tile in range(win.shape[0]):
        cols = pl.ds(tile * LANES, LANES)
        tap = [jnp.broadcast_to(taps[k : k + 1, cols], (SUB, LANES)) for k in range(CONV)]
        near = {
            u: win[tile, pl.ds(offset + u, SUB, stride=SPAN), :] for u in range(1 - CONV, SPAN + CONV - 1)
        }
        for v in range(SPAN):
            centre = tap[CONV - 1] * near[v]
            halves = []
            for sign in (-1, 1):
                total = centre
                for d in range(1, CONV):
                    term = tap[CONV - 1 - d] * near[v + sign * d]
                    if room is not None:
                        left = jnp.broadcast_to(room[sign > 0][:, v : v + 1], (SUB, LANES))
                        term = jnp.where(left >= d, term, 0.0)
                    total = total + term
                halves.append(total * jnp.tanh(total) + total)
            put(tile, pl.ds(v, SUB, stride=SPAN), halves[0], halves[1])


def convolve_block(win, offset, taps, starts, first, put):
    convolve(win, offset, taps, None, put)

    @pl.when(has_cut(starts, first - (CONV - 2), first + BLOCK + CONV - 2))
    def _():
        shape = (SUB, LANES)
        rows = first + iota(shape, 0) * SPAN + iota(shape, 1)
        begin, end = piece_bounds(starts, rows)
        room = ((rows - begin).astype(f32), (end - 1 - rows).astype(f32))
        convolve(win, offset, taps, room, put)


def softplus(x):
    return jnp.maximum(x, 0.0) + jnp.log1p(jnp.exp(-jnp.abs(x)))


def project_kernel(inner, heads, hidden, gain, value_w, state_w, step_w, bias, mix, steps, joined, row):
    @pl.when(pl.program_id(0) == 0)
    def _():
        joined[:, :inner] = value_w[...]
        joined[:, inner : inner + STATE] = state_w[...]
        rows = jnp.concatenate(
            [step_w[...].astype(f32), jnp.zeros((LANES - heads, step_w.shape[1]), f32)], axis=0
        )
        joined[:, inner + STATE :] = jnp.transpose(rows).astype(bf16)
        row[...] = jnp.zeros_like(row)
        row[:, :heads] = bias[...]

    normed = normalise(hidden[...], gain[...].astype(f32))
    out = dot(normed, joined[...])
    mix[...] = out[:, : inner + STATE].astype(bf16)
    steps[...] = softplus(out[:, inner + STATE :] + row[...])


def state_kernel(
    inner,
    heads,
    pieces,
    places,
    lengths,
    info,
    mix,
    before,
    after,
    halo_before,
    halo_after,
    gain,
    value_w,
    state_w,
    steps,
    decay_log,
    conv_value,
    conv_state,
    ends,
    begins,
    passes,
    sent,
    edge,
    win,
    xf,
    xb,
    sums,
    total_f,
    total_b,
    taps,
    rate,
    pick,
):
    quarter = pl.program_id(0)
    quarters = pl.num_programs(0)
    rows = mix.shape[0]
    blocks = rows // BLOCK
    value_tiles = inner // LANES
    starts = bounds_of(lengths, pieces)
    first = info[0] + quarter * rows

    @pl.when(quarter == 0)
    def _():
        for k, halo in enumerate((halo_before, halo_after)):
            normed = normalise(halo[...], gain[...].astype(f32))
            at = pl.ds(k * HALO, HALO)
            edge[at, :inner] = dot(normed, value_w[...]).astype(bf16).astype(f32)
            edge[at, inner:] = dot(normed, state_w[...]).astype(bf16).astype(f32)
        total_f[...] = jnp.zeros_like(total_f)
        total_b[...] = jnp.zeros_like(total_b)
        total_b[STATE : STATE + 1] = jnp.ones((1, inner), f32)
        total_f[STATE : STATE + 1] = jnp.ones((1, inner), f32)
        taps[:, :inner] = conv_value[...].astype(f32) * 0.5
        taps[:, inner:] = conv_state[...].astype(f32) * 0.5
        rate[...] = jnp.zeros_like(rate)
        rate[:, :heads] = jnp.exp(decay_log[...])
        pick[...] = picks(0, inner)

    total = jnp.zeros((1, LANES), f32)
    for c in range(blocks):
        part = running_sum(-steps[pl.ds(c * BLOCK, BLOCK), :] * rate[...]) + total
        sums[pl.ds(c * BLOCK, BLOCK), :] = part
        total = part[BLOCK - 1 : BLOCK]

    last_start = start_at(starts, first + rows - 1)
    first_end = start_after(starts, first)

    end_state = jnp.zeros((STATE, inner), f32)
    begin_state = jnp.zeros((STATE, inner), f32)
    for c in range(blocks):
        at = pl.ds(c * BLOCK, BLOCK)
        tile_up(win, pl.ds(HALO, BLOCK), mix[at, :].astype(f32))
        if c == 0:
            ahead = jnp.where(quarter == 0, edge[:HALO], before[...].astype(f32))
        else:
            ahead = mix[c * BLOCK - HALO : c * BLOCK, :].astype(f32)
        if c == blocks - 1:
            behind = jnp.where(quarter == quarters - 1, edge[HALO:], after[...].astype(f32))
        else:
            behind = mix[(c + 1) * BLOCK : (c + 1) * BLOCK + HALO, :].astype(f32)

        tile_up(win, pl.ds(0, HALO), ahead)
        tile_up(win, pl.ds(HALO + BLOCK, HALO), behind)

        def put(tile, at, forward, backward):
            xf[tile, at, :] = forward
            xb[tile, at, :] = backward

        here = first + c * BLOCK
        convolve_block(win, 0, taps, starts, here, put)
        dt = steps[at, :]
        inclusive = sums[at, :]
        weight_f = dt * jnp.exp(total - inclusive)
        weight_b = dt * jnp.exp(inclusive + dt * rate[...])
        position = iota((BLOCK, 1), 0) + here
        spread_f = dot(halves_of(weight_f), pick[...])
        spread_b = dot(halves_of(weight_b), pick[...])
        write_f = jnp.where(position >= last_start, xf[value_tiles, :BLOCK], 0.0).astype(bf16)
        write_b = jnp.where(position < first_end, xb[value_tiles, :BLOCK], 0.0).astype(bf16)
        end_state += dot_first(write_f, (side_by_side(xf.at[:value_tiles]) * spread_f).astype(bf16))
        begin_state += dot_first(write_b, (side_by_side(xb.at[:value_tiles]) * spread_b).astype(bf16))

    ends[0] = end_state
    begins[0] = begin_state
    decay = dot(halves_of(jnp.broadcast_to(jnp.exp(total), (SUB, LANES))), pick[...])
    pass_f = jnp.where(last_start < first, decay, 0.0)
    pass_b = jnp.where(first_end > first + rows, decay, 0.0)
    passes[0, :8] = pass_f
    passes[0, 8:] = pass_b
    through_f = total_f[STATE : STATE + 1]
    through_b = total_b[STATE : STATE + 1]
    total_f[:STATE] = pass_f[:1] * total_f[:STATE] + end_state
    total_b[:STATE] = total_b[:STATE] + through_b * begin_state
    total_f[STATE : STATE + 1] = through_f * pass_f[:1]
    total_b[STATE : STATE + 1] = through_b * pass_b[:1]

    @pl.when(quarter == quarters - 1)
    def _():
        place = info[1]
        for total_ref, later in ((total_f, True), (total_b, False)):
            state = total_ref[:STATE].astype(bf16)
            high, low = split_halves(total_ref[STATE : STATE + 1])
            pad = jnp.zeros((HALO - 2, inner), f32)
            extra = jnp.concatenate([high.astype(f32), low.astype(f32), pad], axis=0).astype(bf16)

            def fill(p, carry):
                @pl.when((p > place) if later else (p <= place))
                def _():
                    sent[p, :STATE] = state
                    sent[p, STATE:] = extra

                return carry

            lax.fori_loop(0, places, fill, 0)


def carry_kernel(places, quarters, info, got, ends, begins, passes, out):
    place = info[1]
    shape = ends.shape[1:]

    def step(p, state):
        decay = got[p, STATE : STATE + HALO].astype(f32)
        return (decay[0:1] + decay[1:2]) * state + got[p, :STATE].astype(f32)

    def forward(p, state):
        return step(p, state)

    def backward(p, state):
        return step(places - 1 - p, state)

    state = lax.fori_loop(0, place, forward, jnp.zeros(shape, f32))
    for q in range(quarters):
        out[q, 0] = state.astype(bf16)
        state = passes[q, 0:1] * state + ends[q]
    state = lax.fori_loop(0, places - 1 - place, backward, jnp.zeros(shape, f32))
    for q in reversed(range(quarters)):
        out[q, 1] = state.astype(bf16)
        state = passes[q, 8:9] * state + begins[q]


def shared_kernel(
    groups,
    group_heads,
    pieces,
    lengths,
    info,
    hidden,
    above,
    below,
    halo_before,
    halo_after,
    gain,
    state_w,
    conv_state,
    *refs,
):
    smalls, refs = refs[:groups], refs[groups:]
    (
        normed_out,
        factors,
        reach,
        raw,
        raw_t,
        mix_f,
        mix_b,
        write_f,
        write_b,
        read_f,
        read_b,
        enter_f,
        enter_b,
        flags,
        wide,
        xf,
        xb,
        taps,
        step_w,
    ) = refs
    heads = groups * group_heads
    kinds = LANES // heads
    rows = hidden.shape[0]
    blocks = rows // BLOCK
    me = info[3]
    first = info[2]
    starts = bounds_of(lengths, pieces)
    taps[...] = conv_state[...].astype(f32) * 0.5
    for k in range(kinds):
        for g in range(groups):
            at = k * heads + g * group_heads
            step_w[at : at + group_heads, :] = smalls[g][:group_heads, :]
    bias = jnp.zeros((1, LANES), f32)
    rate = jnp.zeros((1, LANES), f32)
    own_lane = iota((1, LANES), 1) < group_heads
    for g in range(groups):
        at = group_heads + CONV + 2
        one_bias = jnp.where(own_lane, smalls[g][at : at + 1, :LANES], 0.0)
        one_rate = jnp.where(own_lane, jnp.exp(smalls[g][at + 1 : at + 2, :LANES]), 0.0)
        for k in range(kinds):
            shift = k * heads + g * group_heads
            bias += pltpu.roll(one_bias, shift, 1) if shift else one_bias
            rate += pltpu.roll(one_rate, shift, 1) if shift else one_rate
    wide_gain = gain[...].astype(f32)
    normed_out[HALO : HALO + rows, :] = normalise(hidden[...], wide_gain)
    ahead = jnp.where(me == 0, halo_before[...].astype(f32), above[...].astype(f32))
    normed_out[:HALO, :] = normalise(ahead, wide_gain)
    behind = jnp.where(me == groups - 1, halo_after[...].astype(f32), below[...].astype(f32))
    normed_out[HALO + rows :, :] = normalise(behind, wide_gain)
    all_steps = dot_last(normed_out[HALO : HALO + rows, :], step_w[...].astype(bf16))
    tile_up(wide, slice(None), dot(normed_out[...], state_w[...]).astype(bf16).astype(f32))
    kind = lax.div(iota((1, LANES), 1), heads)
    totals = []
    for c in range(blocks):
        at = pl.ds(c * BLOCK, BLOCK)
        dt = softplus(all_steps[c * BLOCK : (c + 1) * BLOCK] + bias)
        log_step = -dt * rate
        upto = running_sum(log_step)
        total = upto[BLOCK - 1 : BLOCK]
        onward = total - upto + log_step
        totals.append(total)
        flags[c] = jnp.where(jnp.max(-total) > SAFE, 1, 0)
        value = jnp.where(kind == 0, upto, jnp.where(kind == 1, dt, jnp.where(kind == 2, onward, total)))
        raw[at, :] = value
        raw_t[c] = jnp.transpose(value)
        power = jnp.where(
            kind == 0, upto, jnp.where(kind == 1, -upto, jnp.where(kind == 2, onward, -onward))
        )
        factor = jnp.exp(jnp.minimum(power, SAFE)) * jnp.where((kind & 1) == 1, dt, 1.0)
        factors[at, :] = halves_of(factor)

    zero = jnp.zeros((1, LANES), f32)
    ahead = [zero]
    for c in range(blocks - 1):
        ahead.append(ahead[-1] + totals[c])
    behind = [zero]
    for c in reversed(range(1, blocks)):
        behind.insert(0, behind[0] + totals[c])
    quarter_end = start_after(starts, first - 1)
    quarter_start = start_at(starts, first + rows)
    for c in range(blocks):
        at = pl.ds(c * BLOCK, BLOCK)
        value = raw[at, :]
        power = jnp.where(kind == 0, value + ahead[c], value + behind[c])
        factor = jnp.where((kind & 1) == 0, jnp.exp(jnp.minimum(power, 0.0)), 0.0)
        reach[at, :] = halves_of(factor)

        here = first + c * BLOCK

        def put(tile, at, forward, backward):
            xf[tile, at, :] = forward
            xb[tile, at, :] = backward

        convolve_block(wide, c * BLOCK, taps, starts, here, put)
        position = iota((BLOCK, 1), 0) + here
        begin, end = piece_bounds(starts, position)
        other = iota((BLOCK, BLOCK), 1) + here
        for x, mix, write, read, enter, ahead_of in (
            (xf, mix_f, write_f, read_f, enter_f, True),
            (xb, mix_b, write_b, read_b, enter_b, False),
        ):
            writes = x[0, :BLOCK]
            reads = x[1, :BLOCK]
            inner_product = dot_last(reads.astype(bf16), writes.astype(bf16))
            if ahead_of:
                allowed = (other <= position) & (other >= begin)
                keep = position >= start_at(starts, here + BLOCK - 1)
                opened = position < start_after(starts, here - 1)
                entered = position < quarter_end
            else:
                allowed = (other >= position) & (other < end)
                keep = position < start_after(starts, here)
                opened = position >= start_at(starts, here + BLOCK)
                entered = position >= quarter_start
            mix[c] = jnp.where(allowed, inner_product, 0.0).astype(bf16)
            write[at, :] = jnp.where(keep, writes, 0.0).astype(bf16)
            read[at, :] = jnp.where(opened, reads, 0.0).astype(bf16)
            enter[at, :] = jnp.where(entered, reads, 0.0).astype(bf16)


def group_kernel(
    group,
    split,
    group_heads,
    heads,
    pieces,
    lengths,
    info,
    flags,
    normed,
    factors,
    raw,
    raw_t,
    mix_f,
    mix_b,
    write_f,
    write_b,
    read_f,
    read_b,
    *refs,
):
    members = len(split)
    count = sum(sum(pair) for pair in split)
    smalls, weights, refs = refs[:members], refs[members : members + count], refs[members + count :]
    out_f, out_b, gate_out, held, sems, win, xf, xb, acc, state_f, state_b, pick, taps, skip = refs
    step = pl.program_id(0)
    copies, owners, at = [], [], 0
    for k, pair in enumerate(split):
        for which, number in enumerate(pair):
            row = 0
            for _ in range(number):
                size = weights[at].shape[0]
                target = held.at[2 * k + which, row : row + size]
                copies.append(pltpu.make_async_copy(weights[at], target, sems.at[at]))
                owners.append(k)
                row += size
                at += 1

    @pl.when(step == 0)
    def _():
        for copy in copies:
            copy.start()

    out_f, out_b, gate_out = (r.at[0] for r in (out_f, out_b, gate_out))
    value_w, gate_w = held.at[2 * step], held.at[2 * step + 1]
    inner = held.shape[2]
    rows = out_f.shape[0]
    blocks = rows // BLOCK
    first = info[2]
    starts = bounds_of(lengths, pieces)
    offset = (step + group) * group_heads
    for kind in range(pick.shape[0]):
        pick[kind] = picks(kind * heads + offset, inner)
    for k in range(members):

        @pl.when(step == k)
        def _():
            taps[...] = smalls[k][group_heads : group_heads + CONV, :inner] * 0.5
            skip[...] = smalls[k][group_heads + CONV + 1 : group_heads + CONV + 2, :inner]
            for copy, owner in zip(copies, owners):
                if owner == k:
                    copy.wait()

    tile_up(win, slice(None), dot(normed[...], value_w[...]).astype(bf16).astype(f32))

    def prepare(c, unused):
        at = pl.ds(pl.multiple_of(c * BLOCK, BLOCK), BLOCK)
        centre = normed[pl.ds(pl.multiple_of(c * BLOCK, BLOCK) + HALO, BLOCK), :]
        gate = dot(centre, gate_w[...]).astype(bf16).astype(f32) * 0.5
        gate_out[at, :] = (gate * jnp.tanh(gate) + gate).astype(bf16)

        def put(tile, at, forward, backward):
            xf[c, tile, at, :] = forward
            xb[c, tile, at, :] = backward

        convolve_block(win, c * BLOCK, taps, starts, first + c * BLOCK, put)
        return unused

    lax.fori_loop(0, blocks, prepare, 0)
    state_f[0] = jnp.zeros(state_f.shape[1:], f32)
    state_b[0] = jnp.zeros(state_b.shape[1:], f32)

    ways = (
        (xf, mix_f, write_f, read_f, out_f, state_f, 0, BLOCK - 1),
        (xb, mix_b, write_b, read_b, out_b, state_b, 2, 0),
    )

    def quick(way, c, now, passing):
        x, mix, write, read, out, state, kind, edge_row = way
        at = pl.ds(pl.multiple_of(c * BLOCK, BLOCK), BLOCK)
        here_factors = factors[at, :]
        grow = dot(here_factors, pick[kind])
        carried = state[now]
        values = side_by_side(x.at[c])
        scaled = (values * dot(here_factors, pick[kind + 1])).astype(bf16)
        total = dot(mix[c], scaled) + dot(read[at, :], carried.astype(bf16))
        out[at, :] = (total * grow + skip[...] * values).astype(bf16)
        through = jnp.where(passing, 1.0, 0.0)
        fresh = dot_first(write[at, :], scaled)
        state[1 - now] = grow[edge_row : edge_row + 1] * (fresh + through * carried)

    def general(way, c, now, passing):
        x, mix, write, read, out, state, kind, edge_row = way
        at = pl.ds(pl.multiple_of(c * BLOCK, BLOCK), BLOCK)
        grow = dot(factors[at, :], pick[kind])
        carried = state[now]
        pairs = mix[c].astype(f32)
        lane = iota((1, LANES), 1)
        half = lane >= HEAD_DIM
        values = raw[at, :]

        def pair(p, unused):
            cols = pl.ds(pl.multiple_of(p * LANES, LANES), LANES)
            x_pair = x[c, p, :BLOCK].astype(bf16)
            sums = []
            for side in range(LANES // HEAD_DIM):
                head = offset + p * (LANES // HEAD_DIM) + side
                down = jnp.sum(jnp.where(lane == head + kind * heads, values, 0.0), axis=1, keepdims=True)
                across = raw_t[c, pl.ds(head + kind * heads, 1), :]
                head_steps = raw_t[c, pl.ds(head + heads, 1), :]
                table = pairs * jnp.exp(jnp.minimum(down - across, 0.0)) * head_steps
                sums.append(dot(table.astype(bf16), x_pair))
            acc[:, cols] = jnp.where(half, sums[1], sums[0])
            return unused

        lax.fori_loop(0, inner // LANES, pair, 0)
        wide = side_by_side(x.at[c])
        from_state = dot(read[at, :], carried.astype(bf16))
        out[at, :] = (acc[...] + grow * from_state + skip[...] * wide).astype(bf16)
        head_steps = pltpu.roll(values, (kind - 1) * heads % LANES, 1)
        gap = jnp.minimum(values[edge_row : edge_row + 1] - values, 0.0)
        weight = jnp.where(lax.div(lane, heads) == kind, head_steps * jnp.exp(gap), 0.0)
        scaled = (wide * dot(halves_of(weight), pick[kind])).astype(bf16)
        through = jnp.where(passing, 1.0, 0.0)
        decay = grow[edge_row : edge_row + 1]
        state[1 - now] = dot_first(write[at, :], scaled) + through * decay * carried

    def both(k, unused):
        now = k & 1
        spots = []
        for way, c in zip(ways, (k, blocks - 1 - k)):
            here = first + c * BLOCK
            if way is ways[0]:
                passing = start_at(starts, here + BLOCK - 1) < here
            else:
                passing = start_after(starts, here) > here + BLOCK
            spots.append((way, c, now, passing))
        for spot in spots:
            quick(*spot)
        for spot in spots:

            @pl.when(flags[spot[1]] != 0)
            def _():
                general(*spot)

        return unused

    lax.fori_loop(0, blocks, both, 0)


def finish_kernel(split, group_heads, heads, info, *refs):
    groups = len(split)
    hidden, reach, enter_f, enter_b, carries = refs[:5]
    gains, refs = refs[5 : 5 + groups], refs[5 + groups :]
    gain_row = group_heads + CONV
    tile = hidden.shape[0]
    out_f, out_b, gates = (refs[k * groups : (k + 1) * groups] for k in range(3))
    weights = refs[3 * groups : 3 * groups + sum(split)]
    out, held_f, held_b = refs[3 * groups + sum(split) :]
    me = info[3]
    inner = out_f[0].shape[2]
    here_reach = reach[...]
    sums = [jnp.zeros((tile, 1), f32), jnp.zeros((tile, 1), f32)]
    for g in range(groups):
        gate = gates[g][0].astype(f32)
        for k, (base, enter, held) in enumerate(((out_f, enter_f, held_f), (out_b, enter_b, held_b))):
            grow = dot(here_reach, picks(2 * k * heads + g * group_heads, inner))
            full = base[g][0].astype(f32) + grow * dot(enter[...], carries[me ^ g, k])
            gated = full * gate
            held[:, g * inner : (g + 1) * inner] = gated
            sums[k] = sums[k] + jnp.sum(gated * gated, axis=1, keepdims=True)
    scale_f, scale_b = (lax.rsqrt(s / (groups * inner) + EPSILON) for s in sums)
    total = hidden[...].astype(f32)
    for g in range(groups):
        cols = slice(g * inner, (g + 1) * inner)
        combined = (held_f[:, cols] * scale_f + held_b[:, cols] * scale_b) * gains[g][gain_row : gain_row + 1, :inner]
        combined = combined.astype(bf16)
        row = 0
        for weight in weights[sum(split[:g]) : sum(split[: g + 1])]:
            size = weight.shape[0]
            total = total + dot(combined[:, row : row + size], weight[...])
            row += size
    out[...] = total.astype(bf16)


def whole(shape):
    return pl.BlockSpec(shape, lambda *_: (0,) * len(shape))


def struct(shape, dtype):
    return jax.ShapeDtypeStruct(shape, dtype)


def call(kernel, grid, scalars, arrays, in_specs, out_shape, out_specs, scratch, name):
    return pl.pallas_call(
        kernel,
        grid_spec=pltpu.PrefetchScalarGridSpec(
            num_scalar_prefetch=len(scalars),
            grid=grid,
            in_specs=in_specs,
            out_specs=out_specs,
            scratch_shapes=scratch,
        ),
        out_shape=out_shape,
        compiler_params=pltpu.CompilerParams(
            dimension_semantics=("arbitrary",) * len(grid), vmem_limit_bytes=VMEM_LIMIT
        ),
        name=name,
    )(*scalars, *arrays)


def swap(x, axis, distance):
    return lax.ppermute(x, axis, [(i, i ^ distance) for i in range(lax.axis_size(axis))])


def from_far(x, groups):
    return {k: swap(x, "head", k) for k in range(2, groups, 2)}


def gather_near(x, far, groups):
    held = [[x]] + [None] * (groups - 1)
    for k in range(2, groups, 2):
        held[k] = [part[k] for part in far]
    for k in range(1, groups, 2):
        held[k] = [swap(part, "head", 1) for part in held[k - 1]]
    return held


def cut_rows(x):
    middle = x.shape[0] // 2
    return x[:middle], x[middle:]


def local(
    hidden_in,
    norm_gain,
    gate_weight,
    value_weight,
    state_weight,
    step_weight,
    step_bias,
    decay_log,
    skip_gain,
    conv_value,
    conv_state,
    output_gain,
    output_weight,
    piece_lengths,
):
    tokens, width = hidden_in.shape
    group_heads = step_bias.shape[0]
    inner = value_weight.shape[1]
    groups = lax.axis_size("head")
    places = lax.axis_size("seq")
    heads = group_heads * groups
    me = lax.axis_index("head")
    place = lax.axis_index("seq")
    rows = tokens // groups
    blocks = rows // BLOCK
    pieces = piece_lengths.shape[0]

    up = [(i, i + 1) for i in range(places - 1)]
    down = [(i + 1, i) for i in range(places - 1)]
    before = lax.ppermute(hidden_in[-HALO:], "seq", up)
    after = lax.ppermute(hidden_in[:HALO], "seq", down)
    small = [step_weight.T, conv_value, output_gain.reshape(1, -1)]
    small += [jnp.repeat(skip_gain, HEAD_DIM).reshape(1, -1), step_bias.reshape(1, -1)]
    small += [decay_log.reshape(1, -1)]
    small = jnp.concatenate(
        [jnp.pad(a.astype(f32), ((0, 0), (0, width - a.shape[1]))) for a in small], axis=0
    )
    far_smalls = from_far(small, groups)
    value_first, value_second = cut_rows(value_weight)
    far_first = from_far(value_first, groups)
    info = jnp.stack([place * tokens, place, place * tokens + me * rows, me]).astype(jnp.int32)
    gain = norm_gain.reshape(1, width)

    tile = min(1024, rows)
    columns = inner + STATE
    mix, steps = call(
        functools.partial(project_kernel, inner, group_heads),
        (tokens // tile,),
        (),
        (hidden_in, gain, value_weight, state_weight, step_weight.T, step_bias.reshape(1, -1)),
        [
            pl.BlockSpec((tile, width), lambda i: (i, 0)),
            whole((1, width)),
            whole((width, inner)),
            whole((width, STATE)),
            whole((group_heads, width)),
            whole((1, group_heads)),
        ],
        [struct((tokens, columns), bf16), struct((tokens, LANES), f32)],
        [pl.BlockSpec((tile, columns), lambda i: (i, 0)), pl.BlockSpec((tile, LANES), lambda i: (i, 0))],
        [pltpu.VMEM((width, columns + LANES), bf16), pltpu.VMEM((1, LANES), f32)],
        "project",
    )
    before, after, far_smalls, far_first, value_second, mix = lax.optimization_barrier(
        (before, after, far_smalls, far_first, value_second, mix)
    )
    far_second = from_far(value_second, groups)
    per = rows // HALO
    state_shape = (groups, STATE, inner)
    one_state = pl.BlockSpec((1, STATE, inner), lambda i, *_: (i, 0, 0))
    ends, begins, passes, sent = call(
        functools.partial(state_kernel, inner, group_heads, pieces, places),
        (groups,),
        (piece_lengths, info),
        (
            mix,
            mix,
            mix,
            before,
            after,
            gain,
            value_weight,
            state_weight,
            steps,
            decay_log.reshape(1, -1),
            conv_value,
            conv_state,
        ),
        [
            pl.BlockSpec((rows, columns), lambda i, *_: (i, 0)),
            pl.BlockSpec((HALO, columns), lambda i, *_: (jnp.maximum(i * per - 1, 0), 0)),
            pl.BlockSpec(
                (HALO, columns), lambda i, *_: (jnp.minimum((i + 1) * per, tokens // HALO - 1), 0)
            ),
            whole((HALO, width)),
            whole((HALO, width)),
            whole((1, width)),
            whole((width, inner)),
            whole((width, STATE)),
            pl.BlockSpec((rows, LANES), lambda i, *_: (i, 0)),
            whole((1, group_heads)),
            whole((CONV, inner)),
            whole((CONV, STATE)),
        ],
        [
            struct(state_shape, f32),
            struct(state_shape, f32),
            struct((groups, 2 * SUB, inner), f32),
            struct((places, STATE + HALO, inner), bf16),
        ],
        [
            one_state,
            one_state,
            pl.BlockSpec((1, 2 * SUB, inner), lambda i, *_: (i, 0, 0)),
            whole((places, STATE + HALO, inner)),
        ],
        [
            pltpu.VMEM((2 * HALO, columns), f32),
            pltpu.VMEM((columns // LANES, WINDOW, LANES), f32),
            pltpu.VMEM((columns // LANES, COVER, LANES), f32),
            pltpu.VMEM((columns // LANES, COVER, LANES), f32),
            pltpu.VMEM((rows, LANES), f32),
            pltpu.VMEM((STATE + SUB, inner), f32),
            pltpu.VMEM((STATE + SUB, inner), f32),
            pltpu.VMEM((CONV, columns), f32),
            pltpu.VMEM((1, LANES), f32),
            pltpu.VMEM((2 * LANES, inner), bf16),
        ],
        "states",
    )

    far_second, sent, gate_weight, output_weight = lax.optimization_barrier(
        (far_second, sent, gate_weight, output_weight)
    )
    values = gather_near(value_weight, [far_first, far_second], groups)
    smalls = [piece[0] for piece in gather_near(small, [far_smalls], groups)]
    far_gates = from_far(gate_weight, groups)
    out_first, out_second = cut_rows(output_weight)
    far_out_first = from_far(out_first, groups)
    got = lax.all_to_all(sent, "seq", split_axis=0, concat_axis=0, tiled=True)

    near_shape = (rows + 2 * HALO, width)
    square = struct((blocks, BLOCK, BLOCK), bf16)
    thin = struct((rows, STATE), bf16)
    shapes = [
        struct(near_shape, bf16),
        struct((rows, 2 * LANES), bf16),
        struct((rows, 2 * LANES), bf16),
        struct((rows, LANES), f32),
        struct((blocks, LANES, BLOCK), f32),
        square,
        square,
        thin,
        thin,
        thin,
        thin,
        thin,
        thin,
        struct((blocks,), jnp.int32),
    ]
    shared = call(
        functools.partial(shared_kernel, groups, group_heads, pieces),
        (1,),
        (piece_lengths, info),
        (hidden_in, hidden_in, hidden_in, before, after, gain, state_weight, conv_state, *smalls),
        [
            pl.BlockSpec((rows, width), lambda i, l, at: (at[3], 0)),
            pl.BlockSpec((HALO, width), lambda i, l, at: (jnp.maximum(at[3] * per - 1, 0), 0)),
            pl.BlockSpec(
                (HALO, width), lambda i, l, at: (jnp.minimum((at[3] + 1) * per, tokens // HALO - 1), 0)
            ),
            whole((HALO, width)),
            whole((HALO, width)),
            whole((1, width)),
            whole((width, 2 * STATE)),
            whole((CONV, 2 * STATE)),
        ]
        + [whole(small.shape)] * groups,
        shapes,
        [whole(s.shape) for s in shapes[:-1]] + [pl.BlockSpec(memory_space=pltpu.SMEM)],
        [
            pltpu.VMEM((2, rows + 2 * HALO, STATE), f32),
            pltpu.VMEM((2, COVER, STATE), f32),
            pltpu.VMEM((2, COVER, STATE), f32),
            pltpu.VMEM((CONV, 2 * STATE), f32),
            pltpu.VMEM((LANES, width), f32),
        ],
        "shared",
    )
    normed, factors, reach, raw, raw_t, mix_f, mix_b, write_f, write_b, read_f, read_b = shared[:11]
    enter_f, enter_b, flags = shared[11:]
    members = min(2, groups)
    done = []

    def do_groups(g):
        arrays = (normed, factors, raw, raw_t, mix_f, mix_b, write_f, write_b, read_f, read_b)
        arrays += tuple(smalls[g : g + members])
        loaded = [values[k] + gates[k] for k in range(g, g + members)]
        split = [(len(values[k]), len(gates[k])) for k in range(g, g + members)]
        loaded = [w for ws in loaded for w in ws]
        done.append(
            call(
                functools.partial(group_kernel, g, split, group_heads, heads, pieces),
                (members,),
                (piece_lengths, info, flags),
                arrays + tuple(loaded),
                [whole(a.shape) for a in arrays] + [pl.BlockSpec(memory_space=pl.ANY)] * len(loaded),
                [struct((members, rows, inner), bf16)] * 3,
                [pl.BlockSpec((1, rows, inner), lambda i, *_: (i, 0, 0))] * 3,
                [
                    pltpu.VMEM((2 * members, width, inner), bf16),
                    pltpu.SemaphoreType.DMA((len(loaded),)),
                    pltpu.VMEM((inner // LANES, rows + 2 * HALO, LANES), f32),
                    pltpu.VMEM((blocks, inner // LANES, COVER, LANES), f32),
                    pltpu.VMEM((blocks, inner // LANES, COVER, LANES), f32),
                    pltpu.VMEM((BLOCK, inner), f32),
                    pltpu.VMEM((2, STATE, inner), f32),
                    pltpu.VMEM((2, STATE, inner), f32),
                    pltpu.VMEM((LANES // heads, 2 * LANES, inner), bf16),
                    pltpu.VMEM((CONV, inner), f32),
                    pltpu.VMEM((1, inner), f32),
                ],
                "group%d" % g,
            )
        )

    gates = [[gate_weight], [swap(gate_weight, "head", 1)]][:groups]
    do_groups(0)
    got, done[0], far_out_first, far_gates, out_second = lax.optimization_barrier(
        (got, done[0], far_out_first, far_gates, out_second)
    )
    gates += gather_near(gate_weight, [far_gates], groups)[members:]
    far_out_second = from_far(out_second, groups)
    entering = call(
        functools.partial(carry_kernel, places, groups),
        (1,),
        (info,),
        (got, ends, begins, passes),
        [whole(a.shape) for a in (got, ends, begins, passes)],
        struct((groups, 2, STATE, inner), bf16),
        whole((groups, 2, STATE, inner)),
        [],
        "carries",
    )
    carries = lax.all_to_all(entering, "head", split_axis=0, concat_axis=0, tiled=True)

    for g in range(members, groups, members):
        do_groups(g)
    outs = gather_near(output_weight, [far_out_first, far_out_second], groups)

    tile = min(512, rows)
    tiles = rows // tile

    def by_tile(columns):
        return pl.BlockSpec((tile, columns), lambda i, _: (i, 0))

    def member(k):
        return pl.BlockSpec((1, tile, inner), lambda i, _: (k, i, 0))

    members_of = [(done[g // members], g % members) for g in range(groups)]
    return call(
        functools.partial(finish_kernel, [len(pieces_of) for pieces_of in outs], group_heads, heads),
        (tiles,),
        (info,),
        (hidden_in, reach, enter_f, enter_b, carries, *smalls)
        + tuple(arrays[k] for k in range(3) for arrays, _ in members_of)
        + tuple(piece for pieces_of in outs for piece in pieces_of),
        [
            pl.BlockSpec((tile, width), lambda i, at: (at[3] * tiles + i, 0)),
            by_tile(2 * LANES),
            by_tile(STATE),
            by_tile(STATE),
            whole(carries.shape),
        ]
        + [whole(small.shape)] * groups
        + [member(k) for _, k in members_of] * 3
        + [whole(piece.shape) for pieces_of in outs for piece in pieces_of],
        struct((rows, width), bf16),
        by_tile(width),
        [pltpu.VMEM((tile, groups * inner), f32), pltpu.VMEM((tile, groups * inner), f32)],
        "finish",
    )


def solution(mesh):
    in_specs = (
        P("seq", None),
        P(),
        P(None, "head"),
        P(None, "head"),
        P(),
        P(None, "head"),
        P("head"),
        P("head"),
        P("head"),
        P(None, "head"),
        P(),
        P("head"),
        P("head", None),
        P(),
    )
    out_specs = P(("seq", "head"), None)
    return jax.shard_map(local, mesh=mesh, in_specs=in_specs, out_specs=out_specs, check_vma=False)
```

```python
import functools

import jax
import jax.numpy as jnp
from jax import lax
from jax.experimental import pallas as pl
from jax.experimental.pallas import tpu as pltpu
from jax.sharding import PartitionSpec as P

HEAD_DIM = 64
STATE = 128
CONV = 4
BLOCK = 256
HALO = 16
SUB = 8
SPAN = BLOCK // SUB + 1
COVER = SPAN * SUB
WINDOW = BLOCK + 2 * HALO
LANES = 128
SAFE = 40.0
EPSILON = 1e-05
VMEM_LIMIT = 56 * 1024 * 1024

f32 = jnp.float32
bf16 = jnp.bfloat16


def dot(a, b):
    return jnp.dot(a, b, preferred_element_type=f32)


def dot_first(a, b):
    return lax.dot_general(a, b, (((0,), (0,)), ((), ())), preferred_element_type=f32)


def dot_last(a, b):
    return lax.dot_general(a, b, (((1,), (1,)), ((), ())), preferred_element_type=f32)


def iota(shape, dim):
    return lax.broadcasted_iota(jnp.int32, shape, dim)


def normalise(rows, gain):
    wide = rows.astype(f32)
    scale = lax.rsqrt(jnp.mean(wide * wide, axis=-1, keepdims=True) + EPSILON)
    return (wide * scale * gain).astype(bf16)


def split_halves(x):
    high = x.astype(bf16)
    low = (x - high.astype(f32)).astype(bf16)
    return high, low


def picks(first, columns):
    shape = (2 * LANES, columns)
    pick = (iota(shape, 0) & (LANES - 1)) == lax.div(iota(shape, 1), HEAD_DIM) + first
    return pick.astype(bf16)


def side_by_side(tiles):
    return jnp.concatenate([tiles[k, :BLOCK] for k in range(tiles.shape[0])], axis=1)


def tile_up(tiles, at, x):
    for k in range(tiles.shape[0]):
        tiles[k, at] = x[:, k * LANES : (k + 1) * LANES]


def halves_of(x):
    return jnp.concatenate(split_halves(x), axis=1)


def running_sum(x):
    lower = (iota((BLOCK, BLOCK), 0) >= iota((BLOCK, BLOCK), 1)).astype(bf16)
    high, low = split_halves(x)
    return dot(lower, high) + dot(lower, low)


def bounds_of(lengths, pieces):
    starts = [jnp.int32(0)]
    for k in range(pieces):
        starts.append(starts[-1] + lengths[k])
    return starts


def start_at(starts, row):
    found = starts[0]
    for s in starts[1:]:
        found = jnp.where(s <= row, jnp.maximum(found, s), found)
    return found


def start_after(starts, row):
    found = starts[-1]
    for s in starts[:-1]:
        found = jnp.where(s > row, jnp.minimum(found, s), found)
    return found


def has_cut(starts, low, high):
    found = jnp.int32(0)
    for s in starts:
        found = found | jnp.where((s >= low) & (s <= high), 1, 0)
    return found > 0


def piece_bounds(starts, rows):
    begin = jnp.zeros(rows.shape, jnp.int32)
    end = jnp.zeros(rows.shape, jnp.int32) + starts[-1]
    for s in starts:
        begin = jnp.where(s <= rows, jnp.maximum(begin, s), begin)
        end = jnp.where(s > rows, jnp.minimum(end, s), end)
    return begin, end


def convolve(win, offset, taps, room, put):
    offset = offset + HALO
    for tile in range(win.shape[0]):
        cols = pl.ds(tile * LANES, LANES)
        tap = [jnp.broadcast_to(taps[k : k + 1, cols], (SUB, LANES)) for k in range(CONV)]
        near = {
            u: win[tile, pl.ds(offset + u, SUB, stride=SPAN), :] for u in range(1 - CONV, SPAN + CONV - 1)
        }
        for v in range(SPAN):
            centre = tap[CONV - 1] * near[v]
            halves = []
            for sign in (-1, 1):
                total = centre
                for d in range(1, CONV):
                    term = tap[CONV - 1 - d] * near[v + sign * d]
                    if room is not None:
                        left = jnp.broadcast_to(room[sign > 0][:, v : v + 1], (SUB, LANES))
                        term = jnp.where(left >= d, term, 0.0)
                    total = total + term
                halves.append(total * jnp.tanh(total) + total)
            put(tile, pl.ds(v, SUB, stride=SPAN), halves[0], halves[1])


def convolve_block(win, offset, taps, starts, first, put):
    convolve(win, offset, taps, None, put)
    convolve_cut(win, offset, taps, starts, first, put)


def convolve_cut(win, offset, taps, starts, first, put):
    @pl.when(has_cut(starts, first - (CONV - 2), first + BLOCK + CONV - 2))
    def _():
        shape = (SUB, LANES)
        rows = first + iota(shape, 0) * SPAN + iota(shape, 1)
        begin, end = piece_bounds(starts, rows)
        room = ((rows - begin).astype(f32), (end - 1 - rows).astype(f32))
        convolve(win, offset, taps, room, put)


def softplus(x):
    return jnp.maximum(x, 0.0) + jnp.log1p(jnp.exp(-jnp.abs(x)))


def project_kernel(inner, heads, hidden, gain, value_w, state_w, step_w, bias, mix, steps, joined, row):
    @pl.when(pl.program_id(0) == 0)
    def _():
        joined[:, :inner] = value_w[...]
        joined[:, inner : inner + STATE] = state_w[...]
        rows = jnp.concatenate(
            [step_w[...].astype(f32), jnp.zeros((LANES - heads, step_w.shape[1]), f32)], axis=0
        )
        joined[:, inner + STATE :] = jnp.transpose(rows).astype(bf16)
        row[...] = jnp.zeros_like(row)
        row[:, :heads] = bias[...]

    normed = normalise(hidden[...], gain[...].astype(f32))
    out = dot(normed, joined[...])
    mix[...] = out[:, : inner + STATE].astype(bf16)
    steps[...] = softplus(out[:, inner + STATE :] + row[...])


def pack_kernel(heads, inner, step_w, conv, gain, skip, bias, decay_log, out):
    out[...] = jnp.zeros_like(out)
    out[:heads, :] = step_w[...].astype(f32)
    out[heads : heads + CONV, :inner] = conv[...].astype(f32)
    row = heads + CONV
    out[row : row + 1, :inner] = gain[...].astype(f32)
    wide = jnp.zeros((1, inner), f32)
    head = lax.div(iota((1, inner), 1), HEAD_DIM)
    for h in range(heads):
        wide = jnp.where(head == h, jnp.broadcast_to(skip[:, h : h + 1], (1, inner)), wide)
    out[row + 1 : row + 2, :inner] = wide
    out[row + 2 : row + 3, :heads] = bias[...]
    out[row + 3 : row + 4, :heads] = decay_log[...]


def state_kernel(
    inner,
    heads,
    pieces,
    places,
    lengths,
    info,
    mix,
    before,
    after,
    halo_before,
    halo_after,
    gain,
    value_w,
    state_w,
    steps,
    decay_log,
    conv_value,
    conv_state,
    ends,
    begins,
    passes,
    sent,
    edge,
    win,
    xf,
    xb,
    sums,
    total_f,
    total_b,
    taps,
    rate,
    pick,
):
    quarter = pl.program_id(0)
    quarters = pl.num_programs(0)
    rows = mix.shape[0]
    blocks = rows // BLOCK
    value_tiles = inner // LANES
    starts = bounds_of(lengths, pieces)
    first = info[0] + quarter * rows

    @pl.when(quarter == 0)
    def _():
        for k, halo in enumerate((halo_before, halo_after)):
            normed = normalise(halo[...], gain[...].astype(f32))
            at = pl.ds(k * HALO, HALO)
            edge[at, :inner] = dot(normed, value_w[...]).astype(bf16).astype(f32)
            edge[at, inner:] = dot(normed, state_w[...]).astype(bf16).astype(f32)
        total_f[...] = jnp.zeros_like(total_f)
        total_b[...] = jnp.zeros_like(total_b)
        total_b[STATE : STATE + 1] = jnp.ones((1, inner), f32)
        total_f[STATE : STATE + 1] = jnp.ones((1, inner), f32)
        taps[:, :inner] = conv_value[...].astype(f32) * 0.5
        taps[:, inner:] = conv_state[...].astype(f32) * 0.5
        rate[...] = jnp.zeros_like(rate)
        rate[:, :heads] = jnp.exp(decay_log[...])
        pick[...] = picks(0, inner)

    total = jnp.zeros((1, LANES), f32)
    for c in range(blocks):
        part = running_sum(-steps[pl.ds(c * BLOCK, BLOCK), :] * rate[...]) + total
        sums[pl.ds(c * BLOCK, BLOCK), :] = part
        total = part[BLOCK - 1 : BLOCK]

    last_start = start_at(starts, first + rows - 1)
    first_end = start_after(starts, first)

    end_state = jnp.zeros((STATE, inner), f32)
    begin_state = jnp.zeros((STATE, inner), f32)
    def prepare(c):
        slot = c & 1
        here_win = win.at[slot]
        tile_up(here_win, pl.ds(HALO, BLOCK), mix[pl.ds(c * BLOCK, BLOCK), :].astype(f32))
        if c == 0:
            ahead = jnp.where(quarter == 0, edge[:HALO], before[...].astype(f32))
        else:
            ahead = mix[c * BLOCK - HALO : c * BLOCK, :].astype(f32)
        if c == blocks - 1:
            behind = jnp.where(quarter == quarters - 1, edge[HALO:], after[...].astype(f32))
        else:
            behind = mix[(c + 1) * BLOCK : (c + 1) * BLOCK + HALO, :].astype(f32)
        tile_up(here_win, pl.ds(0, HALO), ahead)
        tile_up(here_win, pl.ds(HALO + BLOCK, HALO), behind)

        def put(tile, at, forward, backward):
            xf[slot, tile, at, :] = forward
            xb[slot, tile, at, :] = backward

        convolve(here_win, 0, taps, None, put)
        return functools.partial(convolve_cut, here_win, 0, taps, starts, first + c * BLOCK, put)

    prepare(0)()
    for c in range(blocks):
        repair = prepare(c + 1) if c + 1 < blocks else None
        at = pl.ds(c * BLOCK, BLOCK)
        here_f, here_b = xf.at[c & 1], xb.at[c & 1]
        dt = steps[at, :]
        inclusive = sums[at, :]
        weight_f = dt * jnp.exp(total - inclusive)
        weight_b = dt * jnp.exp(inclusive + dt * rate[...])
        position = iota((BLOCK, 1), 0) + first + c * BLOCK
        spread_f = dot(halves_of(weight_f), pick[...])
        spread_b = dot(halves_of(weight_b), pick[...])
        write_f = jnp.where(position >= last_start, here_f[value_tiles, :BLOCK], 0.0).astype(bf16)
        write_b = jnp.where(position < first_end, here_b[value_tiles, :BLOCK], 0.0).astype(bf16)
        end_state += dot_first(write_f, (side_by_side(here_f.at[:value_tiles]) * spread_f).astype(bf16))
        begin_state += dot_first(write_b, (side_by_side(here_b.at[:value_tiles]) * spread_b).astype(bf16))
        if repair is not None:
            repair()

    ends[0] = end_state
    begins[0] = begin_state
    decay = dot(halves_of(jnp.broadcast_to(jnp.exp(total), (SUB, LANES))), pick[...])
    pass_f = jnp.where(last_start < first, decay, 0.0)
    pass_b = jnp.where(first_end > first + rows, decay, 0.0)
    passes[0, :8] = pass_f
    passes[0, 8:] = pass_b
    through_f = total_f[STATE : STATE + 1]
    through_b = total_b[STATE : STATE + 1]
    total_f[:STATE] = pass_f[:1] * total_f[:STATE] + end_state
    total_b[:STATE] = total_b[:STATE] + through_b * begin_state
    total_f[STATE : STATE + 1] = through_f * pass_f[:1]
    total_b[STATE : STATE + 1] = through_b * pass_b[:1]

    @pl.when(quarter == quarters - 1)
    def _():
        place = info[1]
        for total_ref, later in ((total_f, True), (total_b, False)):
            state = total_ref[:STATE].astype(bf16)
            high, low = split_halves(total_ref[STATE : STATE + 1])
            pad = jnp.zeros((HALO - 2, inner), f32)
            extra = jnp.concatenate([high.astype(f32), low.astype(f32), pad], axis=0).astype(bf16)

            def fill(p, carry):
                @pl.when((p > place) if later else (p <= place))
                def _():
                    sent[p, :STATE] = state
                    sent[p, STATE:] = extra

                return carry

            lax.fori_loop(0, places, fill, 0)


def carry_kernel(places, quarters, info, got, ends, begins, passes, out):
    place = info[1]
    shape = ends.shape[1:]

    def step(p, state):
        decay = got[p, STATE : STATE + HALO].astype(f32)
        return (decay[0:1] + decay[1:2]) * state + got[p, :STATE].astype(f32)

    def forward(p, state):
        return step(p, state)

    def backward(p, state):
        return step(places - 1 - p, state)

    state = lax.fori_loop(0, place, forward, jnp.zeros(shape, f32))
    for q in range(quarters):
        out[q, 0] = state.astype(bf16)
        state = passes[q, 0:1] * state + ends[q]
    state = lax.fori_loop(0, places - 1 - place, backward, jnp.zeros(shape, f32))
    for q in reversed(range(quarters)):
        out[q, 1] = state.astype(bf16)
        state = passes[q, 8:9] * state + begins[q]


def shared_kernel(
    groups,
    group_heads,
    pieces,
    lengths,
    info,
    hidden,
    above,
    below,
    halo_before,
    halo_after,
    gain,
    state_w,
    conv_state,
    *refs,
):
    smalls, refs = refs[:groups], refs[groups:]
    (
        normed_out,
        factors,
        reach,
        raw,
        raw_t,
        mix_f,
        mix_b,
        write_f,
        write_b,
        read_f,
        read_b,
        enter_f,
        enter_b,
        flags,
        wide,
        xf,
        xb,
        taps,
        step_w,
    ) = refs
    heads = groups * group_heads
    kinds = LANES // heads
    rows = hidden.shape[0]
    blocks = rows // BLOCK
    me = info[3]
    first = info[2]
    starts = bounds_of(lengths, pieces)
    taps[...] = conv_state[...].astype(f32) * 0.5
    for k in range(kinds):
        for g in range(groups):
            at = k * heads + g * group_heads
            step_w[at : at + group_heads, :] = smalls[g][:group_heads, :]
    bias = jnp.zeros((1, LANES), f32)
    rate = jnp.zeros((1, LANES), f32)
    own_lane = iota((1, LANES), 1) < group_heads
    for g in range(groups):
        at = group_heads + CONV + 2
        one_bias = jnp.where(own_lane, smalls[g][at : at + 1, :LANES], 0.0)
        one_rate = jnp.where(own_lane, jnp.exp(smalls[g][at + 1 : at + 2, :LANES]), 0.0)
        for k in range(kinds):
            shift = k * heads + g * group_heads
            bias += pltpu.roll(one_bias, shift, 1) if shift else one_bias
            rate += pltpu.roll(one_rate, shift, 1) if shift else one_rate
    wide_gain = gain[...].astype(f32)
    normed_out[HALO : HALO + rows, :] = normalise(hidden[...], wide_gain)
    ahead = jnp.where(me == 0, halo_before[...].astype(f32), above[...].astype(f32))
    normed_out[:HALO, :] = normalise(ahead, wide_gain)
    behind = jnp.where(me == groups - 1, halo_after[...].astype(f32), below[...].astype(f32))
    normed_out[HALO + rows :, :] = normalise(behind, wide_gain)
    all_steps = dot_last(normed_out[HALO : HALO + rows, :], step_w[...].astype(bf16))
    tile_up(wide, slice(None), dot(normed_out[...], state_w[...]).astype(bf16).astype(f32))
    kind = lax.div(iota((1, LANES), 1), heads)
    totals = []
    for c in range(blocks):
        at = pl.ds(c * BLOCK, BLOCK)
        dt = softplus(all_steps[c * BLOCK : (c + 1) * BLOCK] + bias)
        log_step = -dt * rate
        upto = running_sum(log_step)
        total = upto[BLOCK - 1 : BLOCK]
        onward = total - upto + log_step
        totals.append(total)
        flags[c] = jnp.where(jnp.max(-total) > SAFE, 1, 0)
        value = jnp.where(kind == 0, upto, jnp.where(kind == 1, dt, jnp.where(kind == 2, onward, total)))
        raw[at, :] = value
        raw_t[c] = jnp.transpose(value)
        power = jnp.where(
            kind == 0, upto, jnp.where(kind == 1, -upto, jnp.where(kind == 2, onward, -onward))
        )
        factor = jnp.exp(jnp.minimum(power, SAFE)) * jnp.where((kind & 1) == 1, dt, 1.0)
        factors[at, :] = halves_of(factor)

    zero = jnp.zeros((1, LANES), f32)
    ahead = [zero]
    for c in range(blocks - 1):
        ahead.append(ahead[-1] + totals[c])
    behind = [zero]
    for c in reversed(range(1, blocks)):
        behind.insert(0, behind[0] + totals[c])
    quarter_end = start_after(starts, first - 1)
    quarter_start = start_at(starts, first + rows)
    for c in range(blocks):
        at = pl.ds(c * BLOCK, BLOCK)
        value = raw[at, :]
        power = jnp.where(kind == 0, value + ahead[c], value + behind[c])
        factor = jnp.where((kind & 1) == 0, jnp.exp(jnp.minimum(power, 0.0)), 0.0)
        reach[at, :] = halves_of(factor)

        here = first + c * BLOCK

        def put(tile, at, forward, backward):
            xf[tile, at, :] = forward
            xb[tile, at, :] = backward

        convolve_block(wide, c * BLOCK, taps, starts, here, put)
        position = iota((BLOCK, 1), 0) + here
        begin, end = piece_bounds(starts, position)
        other = iota((BLOCK, BLOCK), 1) + here
        for x, mix, write, read, enter, ahead_of in (
            (xf, mix_f, write_f, read_f, enter_f, True),
            (xb, mix_b, write_b, read_b, enter_b, False),
        ):
            writes = x[0, :BLOCK]
            reads = x[1, :BLOCK]
            inner_product = dot_last(reads.astype(bf16), writes.astype(bf16))
            if ahead_of:
                allowed = (other <= position) & (other >= begin)
                keep = position >= start_at(starts, here + BLOCK - 1)
                opened = position < start_after(starts, here - 1)
                entered = position < quarter_end
            else:
                allowed = (other >= position) & (other < end)
                keep = position < start_after(starts, here)
                opened = position >= start_at(starts, here + BLOCK)
                entered = position >= quarter_start
            mix[c] = jnp.where(allowed, inner_product, 0.0).astype(bf16)
            write[at, :] = jnp.where(keep, writes, 0.0).astype(bf16)
            read[at, :] = jnp.where(opened, reads, 0.0).astype(bf16)
            enter[at, :] = jnp.where(entered, reads, 0.0).astype(bf16)


def group_kernel(group, split, group_heads, heads, pieces, lengths, info, flags, *refs):
    members = len(split)
    count = sum(sum(pair) for pair in split)
    smalls, refs = refs[:members], refs[members:]
    raw_far, raw_t_far = refs[:2]
    shared_far, refs = refs[2:10], refs[10:]
    weights, refs = refs[:count], refs[count:]
    out_f, out_b, gate_out, held, sems = refs[:5]
    normed, factors, mix_f, mix_b, write_f, write_b, read_f, read_b = refs[5:13]
    raw, raw_t, win, xf, xb, acc, state_f, state_b, pick, taps, skip = refs[13:]
    step = pl.program_id(0)
    copies, at = {}, 0
    for k, pair in enumerate(split):
        for which, number in enumerate(pair):
            row = 0
            copies[k, which] = []
            for _ in range(number):
                size = weights[at].shape[0]
                target = held.at[2 * k + which, row : row + size]
                copies[k, which].append(pltpu.make_async_copy(weights[at], target, sems.at[at]))
                row += size
                at += 1
    near = refs[5:13]
    shared = [
        pltpu.make_async_copy(far, here, sems.at[count + k])
        for k, (far, here) in enumerate(zip(shared_far, near))
    ]

    def start(some):
        for copy in some:
            copy.start()

    def wait(some):
        for copy in some:
            copy.wait()

    @pl.when(step == 0)
    def _():
        start(shared[:1] + copies[0, 0])
        wait(shared[:1] + copies[0, 0])
        start(copies[0, 1] + shared[1:])
        for k in range(1, members):
            start(copies[k, 0] + copies[k, 1])

    for k in range(1, members):

        @pl.when(step == k)
        def _():
            wait(copies[k, 0] + copies[k, 1])

    out_f, out_b, gate_out = (r.at[0] for r in (out_f, out_b, gate_out))
    value_w, gate_w = held.at[2 * step], held.at[2 * step + 1]
    inner = held.shape[2]
    rows = out_f.shape[0]
    blocks = rows // BLOCK
    first = info[2]
    starts = bounds_of(lengths, pieces)
    offset = (step + group) * group_heads
    for kind in range(pick.shape[0]):
        pick[kind] = picks(kind * heads + offset, inner)
    for k in range(members):

        @pl.when(step == k)
        def _():
            taps[...] = smalls[k][group_heads : group_heads + CONV, :inner] * 0.5
            skip[...] = smalls[k][group_heads + CONV + 1 : group_heads + CONV + 2, :inner]

    tile_up(win, slice(None), dot(normed[...], value_w[...]).astype(bf16).astype(f32))

    @pl.when(step == 0)
    def _():
        wait(copies[0, 1] + shared[1:])

    def prepare(c, unused):
        at = pl.ds(pl.multiple_of(c * BLOCK, BLOCK), BLOCK)
        centre = normed[pl.ds(pl.multiple_of(c * BLOCK, BLOCK) + HALO, BLOCK), :]
        gate = dot(centre, gate_w[...]).astype(bf16).astype(f32) * 0.5
        gate_out[at, :] = (gate * jnp.tanh(gate) + gate).astype(bf16)

        def put(tile, at, forward, backward):
            xf[c, tile, at, :] = forward
            xb[c, tile, at, :] = backward

        convolve_block(win, c * BLOCK, taps, starts, first + c * BLOCK, put)
        return unused

    lax.fori_loop(0, blocks, prepare, 0)
    state_f[0] = jnp.zeros(state_f.shape[1:], f32)
    state_b[0] = jnp.zeros(state_b.shape[1:], f32)

    ways = (
        (xf, mix_f, write_f, read_f, out_f, state_f, 0, BLOCK - 1),
        (xb, mix_b, write_b, read_b, out_b, state_b, 2, 0),
    )

    def quick(way, c, now, passing):
        x, mix, write, read, out, state, kind, edge_row = way
        at = pl.ds(pl.multiple_of(c * BLOCK, BLOCK), BLOCK)
        here_factors = factors[at, :]
        grow = dot(here_factors, pick[kind])
        carried = state[now]
        values = side_by_side(x.at[c])
        scaled = (values * dot(here_factors, pick[kind + 1])).astype(bf16)
        total = dot(mix[c], scaled) + dot(read[at, :], carried.astype(bf16))
        out[at, :] = (total * grow + skip[...] * values).astype(bf16)
        through = jnp.where(passing, 1.0, 0.0)
        fresh = dot_first(write[at, :], scaled)
        state[1 - now] = grow[edge_row : edge_row + 1] * (fresh + through * carried)

    def general(way, c, now, passing):
        x, mix, write, read, out, state, kind, edge_row = way
        at = pl.ds(pl.multiple_of(c * BLOCK, BLOCK), BLOCK)
        grow = dot(factors[at, :], pick[kind])
        carried = state[now]
        pltpu.sync_copy(raw_far.at[at, :], raw)
        pltpu.sync_copy(raw_t_far.at[c], raw_t)
        pairs = mix[c].astype(f32)
        lane = iota((1, LANES), 1)
        half = lane >= HEAD_DIM
        values = raw[...]

        def pair(p, unused):
            cols = pl.ds(pl.multiple_of(p * LANES, LANES), LANES)
            x_pair = x[c, p, :BLOCK].astype(bf16)
            sums = []
            for side in range(LANES // HEAD_DIM):
                head = offset + p * (LANES // HEAD_DIM) + side
                down = jnp.sum(jnp.where(lane == head + kind * heads, values, 0.0), axis=1, keepdims=True)
                across = raw_t[pl.ds(head + kind * heads, 1), :]
                head_steps = raw_t[pl.ds(head + heads, 1), :]
                table = pairs * jnp.exp(jnp.minimum(down - across, 0.0)) * head_steps
                sums.append(dot(table.astype(bf16), x_pair))
            acc[:, cols] = jnp.where(half, sums[1], sums[0])
            return unused

        lax.fori_loop(0, inner // LANES, pair, 0)
        wide = side_by_side(x.at[c])
        from_state = dot(read[at, :], carried.astype(bf16))
        out[at, :] = (acc[...] + grow * from_state + skip[...] * wide).astype(bf16)
        head_steps = pltpu.roll(values, (kind - 1) * heads % LANES, 1)
        gap = jnp.minimum(values[edge_row : edge_row + 1] - values, 0.0)
        weight = jnp.where(lax.div(lane, heads) == kind, head_steps * jnp.exp(gap), 0.0)
        scaled = (wide * dot(halves_of(weight), pick[kind])).astype(bf16)
        through = jnp.where(passing, 1.0, 0.0)
        decay = grow[edge_row : edge_row + 1]
        state[1 - now] = dot_first(write[at, :], scaled) + through * decay * carried

    def both(k, unused):
        now = k & 1
        spots = []
        for way, c in zip(ways, (k, blocks - 1 - k)):
            here = first + c * BLOCK
            if way is ways[0]:
                passing = start_at(starts, here + BLOCK - 1) < here
            else:
                passing = start_after(starts, here) > here + BLOCK
            spots.append((way, c, now, passing))
        for spot in spots:
            quick(*spot)
        for spot in spots:

            @pl.when(flags[spot[1]] != 0)
            def _():
                general(*spot)

        return unused

    lax.fori_loop(0, blocks, both, 0)


def finish_kernel(split, group_heads, heads, info, *refs):
    groups = len(split)
    hidden, reach, enter_f, enter_b, carries = refs[:5]
    gains, refs = refs[5 : 5 + groups], refs[5 + groups :]
    gain_row = group_heads + CONV
    tile = hidden.shape[0]
    out_f, out_b, gates = (refs[k * groups : (k + 1) * groups] for k in range(3))
    weights = refs[3 * groups : 3 * groups + sum(split)]
    out, held_f, held_b = refs[3 * groups + sum(split) :]
    me = info[3]
    inner = out_f[0].shape[2]
    here_reach = reach[...]
    sums = [jnp.zeros((tile, 1), f32), jnp.zeros((tile, 1), f32)]
    for g in range(groups):
        gate = gates[g][0].astype(f32)
        for k, (base, enter, held) in enumerate(((out_f, enter_f, held_f), (out_b, enter_b, held_b))):
            grow = dot(here_reach, picks(2 * k * heads + g * group_heads, inner))
            full = base[g][0].astype(f32) + grow * dot(enter[...], carries[me ^ g, k])
            gated = full * gate
            held[:, g * inner : (g + 1) * inner] = gated
            sums[k] = sums[k] + jnp.sum(gated * gated, axis=1, keepdims=True)
    scale_f, scale_b = (lax.rsqrt(s / (groups * inner) + EPSILON) for s in sums)
    total = hidden[...].astype(f32)
    for g in range(groups):
        cols = slice(g * inner, (g + 1) * inner)
        combined = (held_f[:, cols] * scale_f + held_b[:, cols] * scale_b) * gains[g][gain_row : gain_row + 1, :inner]
        combined = combined.astype(bf16)
        row = 0
        for weight in weights[sum(split[:g]) : sum(split[: g + 1])]:
            size = weight.shape[0]
            total = total + dot(combined[:, row : row + size], weight[...])
            row += size
    out[...] = total.astype(bf16)


def whole(shape):
    return pl.BlockSpec(shape, lambda *_: (0,) * len(shape))


def struct(shape, dtype):
    return jax.ShapeDtypeStruct(shape, dtype)


def call(kernel, grid, scalars, arrays, in_specs, out_shape, out_specs, scratch, name):
    return pl.pallas_call(
        kernel,
        grid_spec=pltpu.PrefetchScalarGridSpec(
            num_scalar_prefetch=len(scalars),
            grid=grid,
            in_specs=in_specs,
            out_specs=out_specs,
            scratch_shapes=scratch,
        ),
        out_shape=out_shape,
        compiler_params=pltpu.CompilerParams(
            dimension_semantics=("arbitrary",) * len(grid), vmem_limit_bytes=VMEM_LIMIT
        ),
        name=name,
    )(*scalars, *arrays)


def swap(x, axis, distance):
    return lax.ppermute(x, axis, [(i, i ^ distance) for i in range(lax.axis_size(axis))])


def from_far(x, groups):
    return {k: swap(x, "head", k) for k in range(2, groups, 2)}


def gather_near(x, far, groups):
    held = [[x]] + [None] * (groups - 1)
    for k in range(2, groups, 2):
        held[k] = [part[k] for part in far]
    for k in range(1, groups, 2):
        held[k] = [swap(part, "head", 1) for part in held[k - 1]]
    return held


def local(
    hidden_in,
    norm_gain,
    gate_weight,
    value_weight,
    state_weight,
    step_weight,
    step_bias,
    decay_log,
    skip_gain,
    conv_value,
    conv_state,
    output_gain,
    output_weight,
    piece_lengths,
):
    tokens, width = hidden_in.shape
    group_heads = step_bias.shape[0]
    inner = value_weight.shape[1]
    groups = lax.axis_size("head")
    places = lax.axis_size("seq")
    heads = group_heads * groups
    me = lax.axis_index("head")
    place = lax.axis_index("seq")
    rows = tokens // groups
    blocks = rows // BLOCK
    pieces = piece_lengths.shape[0]

    up = [(i, i + 1) for i in range(places - 1)]
    down = [(i + 1, i) for i in range(places - 1)]
    before = lax.ppermute(hidden_in[-HALO:], "seq", up)
    after = lax.ppermute(hidden_in[:HALO], "seq", down)
    small = [step_weight.T, conv_value, output_gain.reshape(1, -1)]
    small += [a.reshape(1, -1) for a in (skip_gain, step_bias, decay_log)]
    small_rows = -(-(group_heads + CONV + 4) // SUB) * SUB
    small = call(
        functools.partial(pack_kernel, group_heads, inner),
        (1,),
        (),
        small,
        [whole(a.shape) for a in small],
        struct((small_rows, width), f32),
        whole((small_rows, width)),
        [],
        "small",
    )
    far_smalls = from_far(small, groups)
    far_values = from_far(value_weight, groups)
    info = jnp.stack([place * tokens, place, place * tokens + me * rows, me]).astype(jnp.int32)
    gain = norm_gain.reshape(1, width)

    tile = min(1024, rows)
    columns = inner + STATE
    mix, steps = call(
        functools.partial(project_kernel, inner, group_heads),
        (tokens // tile,),
        (),
        (hidden_in, gain, value_weight, state_weight, step_weight.T, step_bias.reshape(1, -1)),
        [
            pl.BlockSpec((tile, width), lambda i: (i, 0)),
            whole((1, width)),
            whole((width, inner)),
            whole((width, STATE)),
            whole((group_heads, width)),
            whole((1, group_heads)),
        ],
        [struct((tokens, columns), bf16), struct((tokens, LANES), f32)],
        [pl.BlockSpec((tile, columns), lambda i: (i, 0)), pl.BlockSpec((tile, LANES), lambda i: (i, 0))],
        [pltpu.VMEM((width, columns + LANES), bf16), pltpu.VMEM((1, LANES), f32)],
        "project",
    )
    before, after, far_smalls, far_values, gate_weight, mix = lax.optimization_barrier(
        (before, after, far_smalls, far_values, gate_weight, mix)
    )
    far_gates = from_far(gate_weight, groups)
    per = rows // HALO
    state_shape = (groups, STATE, inner)
    one_state = pl.BlockSpec((1, STATE, inner), lambda i, *_: (i, 0, 0))
    ends, begins, passes, sent = call(
        functools.partial(state_kernel, inner, group_heads, pieces, places),
        (groups,),
        (piece_lengths, info),
        (
            mix,
            mix,
            mix,
            before,
            after,
            gain,
            value_weight,
            state_weight,
            steps,
            decay_log.reshape(1, -1),
            conv_value,
            conv_state,
        ),
        [
            pl.BlockSpec((rows, columns), lambda i, *_: (i, 0)),
            pl.BlockSpec((HALO, columns), lambda i, *_: (jnp.maximum(i * per - 1, 0), 0)),
            pl.BlockSpec(
                (HALO, columns), lambda i, *_: (jnp.minimum((i + 1) * per, tokens // HALO - 1), 0)
            ),
            whole((HALO, width)),
            whole((HALO, width)),
            whole((1, width)),
            whole((width, inner)),
            whole((width, STATE)),
            pl.BlockSpec((rows, LANES), lambda i, *_: (i, 0)),
            whole((1, group_heads)),
            whole((CONV, inner)),
            whole((CONV, STATE)),
        ],
        [
            struct(state_shape, f32),
            struct(state_shape, f32),
            struct((groups, 2 * SUB, inner), f32),
            struct((places, STATE + HALO, inner), bf16),
        ],
        [
            one_state,
            one_state,
            pl.BlockSpec((1, 2 * SUB, inner), lambda i, *_: (i, 0, 0)),
            whole((places, STATE + HALO, inner)),
        ],
        [
            pltpu.VMEM((2 * HALO, columns), f32),
            pltpu.VMEM((2, columns // LANES, WINDOW, LANES), f32),
            pltpu.VMEM((2, columns // LANES, COVER, LANES), f32),
            pltpu.VMEM((2, columns // LANES, COVER, LANES), f32),
            pltpu.VMEM((rows, LANES), f32),
            pltpu.VMEM((STATE + SUB, inner), f32),
            pltpu.VMEM((STATE + SUB, inner), f32),
            pltpu.VMEM((CONV, columns), f32),
            pltpu.VMEM((1, LANES), f32),
            pltpu.VMEM((2 * LANES, inner), bf16),
        ],
        "states",
    )

    values = gather_near(value_weight, [far_values], groups)
    smalls = [piece[0] for piece in gather_near(small, [far_smalls], groups)]
    far_gates, sent, output_weight, values, smalls = lax.optimization_barrier(
        (far_gates, sent, output_weight, values, smalls)
    )
    far_outs = from_far(output_weight, groups)
    got = lax.all_to_all(sent, "seq", split_axis=0, concat_axis=0, tiled=True)

    near_shape = (rows + 2 * HALO, width)
    square = struct((blocks, BLOCK, BLOCK), bf16)
    thin = struct((rows, STATE), bf16)
    shapes = [
        struct(near_shape, bf16),
        struct((rows, 2 * LANES), bf16),
        struct((rows, 2 * LANES), bf16),
        struct((rows, LANES), f32),
        struct((blocks, LANES, BLOCK), f32),
        square,
        square,
        thin,
        thin,
        thin,
        thin,
        thin,
        thin,
        struct((blocks,), jnp.int32),
    ]
    shared = call(
        functools.partial(shared_kernel, groups, group_heads, pieces),
        (1,),
        (piece_lengths, info),
        (hidden_in, hidden_in, hidden_in, before, after, gain, state_weight, conv_state, *smalls),
        [
            pl.BlockSpec((rows, width), lambda i, l, at: (at[3], 0)),
            pl.BlockSpec((HALO, width), lambda i, l, at: (jnp.maximum(at[3] * per - 1, 0), 0)),
            pl.BlockSpec(
                (HALO, width), lambda i, l, at: (jnp.minimum((at[3] + 1) * per, tokens // HALO - 1), 0)
            ),
            whole((HALO, width)),
            whole((HALO, width)),
            whole((1, width)),
            whole((width, 2 * STATE)),
            whole((CONV, 2 * STATE)),
        ]
        + [whole(small.shape)] * groups,
        shapes,
        [whole(s.shape) for s in shapes[:-1]] + [pl.BlockSpec(memory_space=pltpu.SMEM)],
        [
            pltpu.VMEM((2, rows + 2 * HALO, STATE), f32),
            pltpu.VMEM((2, COVER, STATE), f32),
            pltpu.VMEM((2, COVER, STATE), f32),
            pltpu.VMEM((CONV, 2 * STATE), f32),
            pltpu.VMEM((LANES, width), f32),
        ],
        "shared",
    )
    normed, factors, reach, raw, raw_t, mix_f, mix_b, write_f, write_b, read_f, read_b = shared[:11]
    enter_f, enter_b, flags = shared[11:]
    members = min(2, groups)
    done = []

    def do_groups(g):
        small = tuple(smalls[g : g + members])
        arrays = (normed, factors, mix_f, mix_b, write_f, write_b, read_f, read_b)
        loaded = [values[k] + gates[k] for k in range(g, g + members)]
        split = [(len(values[k]), len(gates[k])) for k in range(g, g + members)]
        loaded = [w for ws in loaded for w in ws]
        done.append(
            call(
                functools.partial(group_kernel, g, split, group_heads, heads, pieces),
                (members,),
                (piece_lengths, info, flags),
                small + (raw, raw_t) + arrays + tuple(loaded),
                [whole(a.shape) for a in small]
                + [pl.BlockSpec(memory_space=pl.ANY)] * (2 + len(arrays) + len(loaded)),
                [struct((members, rows, inner), bf16)] * 3,
                [pl.BlockSpec((1, rows, inner), lambda i, *_: (i, 0, 0))] * 3,
                [
                    pltpu.VMEM((2 * members, width, inner), bf16),
                    pltpu.SemaphoreType.DMA((len(loaded) + len(arrays),)),
                ]
                + [pltpu.VMEM(a.shape, a.dtype) for a in arrays]
                + [
                    pltpu.VMEM((BLOCK, LANES), f32),
                    pltpu.VMEM((LANES, BLOCK), f32),
                    pltpu.VMEM((inner // LANES, rows + 2 * HALO, LANES), f32),
                    pltpu.VMEM((blocks, inner // LANES, COVER, LANES), f32),
                    pltpu.VMEM((blocks, inner // LANES, COVER, LANES), f32),
                    pltpu.VMEM((BLOCK, inner), f32),
                    pltpu.VMEM((2, STATE, inner), f32),
                    pltpu.VMEM((2, STATE, inner), f32),
                    pltpu.VMEM((LANES // heads, 2 * LANES, inner), bf16),
                    pltpu.VMEM((CONV, inner), f32),
                    pltpu.VMEM((1, inner), f32),
                ],
                "group%d" % g,
            )
        )

    gates = [[gate_weight], [swap(gate_weight, "head", 1)]][:groups]
    do_groups(0)
    got, done[0], far_outs = lax.optimization_barrier((got, done[0], far_outs))
    gates += gather_near(gate_weight, [far_gates], groups)[members:]
    entering = call(
        functools.partial(carry_kernel, places, groups),
        (1,),
        (info,),
        (got, ends, begins, passes),
        [whole(a.shape) for a in (got, ends, begins, passes)],
        struct((groups, 2, STATE, inner), bf16),
        whole((groups, 2, STATE, inner)),
        [],
        "carries",
    )
    carries = lax.all_to_all(entering, "head", split_axis=0, concat_axis=0, tiled=True)

    for g in range(members, groups, members):
        do_groups(g)
    outs = gather_near(output_weight, [far_outs], groups)

    tile = min(512, rows)
    tiles = rows // tile

    def by_tile(columns):
        return pl.BlockSpec((tile, columns), lambda i, _: (i, 0))

    def member(k):
        return pl.BlockSpec((1, tile, inner), lambda i, _: (k, i, 0))

    members_of = [(done[g // members], g % members) for g in range(groups)]
    return call(
        functools.partial(finish_kernel, [len(pieces_of) for pieces_of in outs], group_heads, heads),
        (tiles,),
        (info,),
        (hidden_in, reach, enter_f, enter_b, carries, *smalls)
        + tuple(arrays[k] for k in range(3) for arrays, _ in members_of)
        + tuple(piece for pieces_of in outs for piece in pieces_of),
        [
            pl.BlockSpec((tile, width), lambda i, at: (at[3] * tiles + i, 0)),
            by_tile(2 * LANES),
            by_tile(STATE),
            by_tile(STATE),
            whole(carries.shape),
        ]
        + [whole(small.shape)] * groups
        + [member(k) for _, k in members_of] * 3
        + [whole(piece.shape) for pieces_of in outs for piece in pieces_of],
        struct((rows, width), bf16),
        by_tile(width),
        [pltpu.VMEM((tile, groups * inner), f32), pltpu.VMEM((tile, groups * inner), f32)],
        "finish",
    )


def solution(mesh):
    in_specs = (
        P("seq", None),
        P(),
        P(None, "head"),
        P(None, "head"),
        P(),
        P(None, "head"),
        P("head"),
        P("head"),
        P("head"),
        P(None, "head"),
        P(),
        P("head"),
        P("head", None),
        P(),
    )
    out_specs = P(("seq", "head"), None)
    return jax.shard_map(local, mesh=mesh, in_specs=in_specs, out_specs=out_specs, check_vma=False)
```
